32 devices in a mesh: outer: 4 (over z), inner: 4 (over x, core), head: 2 (over y).
Axes of the slice: x: 2, y: 2, z: 4, core: 2. Of those that a mesh axis runs over, the one named last changes fastest.
Arguments:
- query: bfloat16 [2048, 6144], P(('outer', 'inner'), 'head'), may hold values from -6 to 6
- key: bfloat16 [2048, 1024], P(('outer', 'inner', 'head')), may hold values from -6 to 6
- value: bfloat16 [2048, 1024], P(('outer', 'inner', 'head')), may hold values from -6 to 6
- output_cotangent: bfloat16 [2048, 6144], P(('outer', 'inner'), 'head'), may hold values from -6 to 6
- segment: int32 [2048], replicated, may hold values from 0 to 15, never falling along the last dimension, each value on 1 to 256 neighbouring positions
Outputs:
- attended: bfloat16 [2048, 6144], P(('outer', 'inner'), 'head')
- d_query: bfloat16 [2048, 6144], P(('outer', 'inner'), 'head')
- d_key: bfloat16 [2048, 1024], P(('outer', 'inner', 'head'))
- d_value: bfloat16 [2048, 1024], P(('outer', 'inner', 'head'))
The draws below stay inside these ranges and needn't reach their ends.
Inputs may be any that keep to these rules, and one draw needn't show every extreme that they name: `segment`: ids never fall along the row; every document has 1 to 256 tokens, and some document has exactly 256.
All inputs are finite; a program needn't handle non-finite values.
Results may differ from the reference program's by a relative error of at most 0.03.
Values may be sent and summed in bfloat16 or wider, within the bound.
A program may use at most 64 MiB of HBM per device.

```python
import math
import jax
import jax.numpy as jnp
import numpy as np
from jax import lax

QUERY_HEADS = 48
KEY_VALUE_HEADS = 8
HEAD_SIZE = 128
CONTEXT_TOKENS = 128
REACH = 2
ROW_TOKENS = 2048
DOCS = 16


def draw_query(key, part):
    value_rows = jnp.clip(jax.random.normal(jax.random.fold_in(key, 11), (ROW_TOKENS, QUERY_HEADS * HEAD_SIZE), jnp.float32), -6.0, 6.0)
    return value_rows.astype(jnp.bfloat16)


def draw_key(key, part):
    value_rows = jnp.clip(jax.random.normal(jax.random.fold_in(key, 13), (ROW_TOKENS, KEY_VALUE_HEADS * HEAD_SIZE), jnp.float32), -6.0, 6.0)
    return value_rows.astype(jnp.bfloat16)


def block_scale(own_key, extent, pieces, low, top_value):
    def one(position, parts):
        heights = jax.random.uniform(jax.random.fold_in(jax.random.fold_in(own_key, 6), position), (parts,), jnp.float32, low / len(pieces), top_value / len(pieces))
        return jnp.repeat(jnp.exp(heights), extent[position] // parts).reshape((-1,) + (1,) * (len(extent) - position - 1))

    level = one(*pieces[0])
    for cut in pieces[1:]:
        level = level * one(*cut)
    return level


def split_up(number_of, total, most, skew):
    portions = [(1 << 20) // math.isqrt(rank ** skew) + 1 for rank in range(2, number_of + 1)]
    spare, given = total - most - (number_of - 1), [1] * (number_of - 1)
    while spare > 0:
        free = [i for i in range(number_of - 1) if given[i] < most]
        mass, remaining = sum([portions[i] for i in free]), spare
        for i in free:
            addition = min(most - given[i], max(1, remaining * portions[i] // mass), spare)
            given[i] = given[i] + addition
            spare = spare - addition
    return np.array([most] + given)


def ragged_sizes(own_key, amount, total, most, lean):
    if amount == 2:
        one = jax.random.randint(own_key, (), max(1, total - most), min(most, total - 1) + 1)
        return jnp.stack([one, total - one])
    sizes = jnp.asarray(split_up(amount, total, most, lean), jnp.int32)
    couples = (amount - 1) // 2
    giver, receiver = sizes[1:1 + 2 * couples:2], sizes[2:2 + 2 * couples:2]
    slack = jnp.minimum(giver - 1, most - receiver)
    passed = jax.random.randint(jax.random.fold_in(own_key, 1), (couples,), 0, 1 << 20) % (slack + 1)
    sizes = sizes.at[1:1 + 2 * couples:2].set(giver - passed).at[2:2 + 2 * couples:2].set(receiver + passed)
    return sizes[jax.random.permutation(jax.random.fold_in(own_key, 2), amount)]


def centred(key, shape, spread, most, split=(), held_as=jnp.bfloat16):
    factor_of = block_scale(key, shape, split, -0.22, 0.18) if split else 1.0
    entries = jax.random.normal(key, shape, jnp.float32) * spread * factor_of
    return jnp.minimum(jnp.maximum(entries, -most), most).astype(held_as)


def setup_inputs(seed: int = 0) -> dict:
    arg_keys = jax.random.split(jax.random.key(seed), 6)
    query = draw_query(jax.random.fold_in(arg_keys[5], 71), 0)
    key = draw_key(jax.random.fold_in(arg_keys[5], 71), 0)
    value = centred(arg_keys[2], (ROW_TOKENS, KEY_VALUE_HEADS * HEAD_SIZE), 1.0, 6.0, ((0, 32),))
    output_cotangent = centred(arg_keys[3], (ROW_TOKENS, QUERY_HEADS * HEAD_SIZE), 1.0, 6.0, ((0, 16), (1, 2)))
    segment = jnp.searchsorted(jnp.cumsum(ragged_sizes(arg_keys[4], DOCS, ROW_TOKENS, REACH * CONTEXT_TOKENS, 2)), jnp.arange(ROW_TOKENS), side="right").astype(jnp.int32)
    return {"query": query, "key": key, "value": value, "output_cotangent": output_cotangent, "segment": segment}


def rounded(value_rows):
    return lax.optimization_barrier(value_rows.astype(jnp.bfloat16)).astype(jnp.float32)

def reference(query, key, value, output_cotangent, segment):
    query_group_width = QUERY_HEADS // KEY_VALUE_HEADS
    factor = 1.0 / math.sqrt(HEAD_SIZE)
    slice_view = (REACH + 1) * CONTEXT_TOKENS
    pad_amount = REACH * CONTEXT_TOKENS
    padded_keys = jnp.concatenate([jnp.zeros((pad_amount, KEY_VALUE_HEADS * HEAD_SIZE), key.dtype), key], 0)
    padded_values = jnp.concatenate([jnp.zeros((pad_amount, KEY_VALUE_HEADS * HEAD_SIZE), value.dtype), value], 0)
    seg_pad = jnp.concatenate([jnp.full((pad_amount,), -1, jnp.int32), segment.astype(jnp.int32)], 0)
    block_count = ROW_TOKENS // CONTEXT_TOKENS

    def one_block(totals, block_index):
        key_gradient, value_gradient = totals
        row_beginning = (block_index * CONTEXT_TOKENS).astype(jnp.int32)
        query_tile_rows = lax.dynamic_slice_in_dim(query, row_beginning, CONTEXT_TOKENS, 0).astype(jnp.float32).reshape(CONTEXT_TOKENS, KEY_VALUE_HEADS, query_group_width, HEAD_SIZE)
        block_gradients = lax.dynamic_slice_in_dim(output_cotangent, row_beginning, CONTEXT_TOKENS, 0).astype(jnp.float32).reshape(CONTEXT_TOKENS, KEY_VALUE_HEADS, query_group_width, HEAD_SIZE)
        key_slice_view = lax.dynamic_slice_in_dim(padded_keys, row_beginning, slice_view, 0).astype(jnp.float32).reshape(slice_view, KEY_VALUE_HEADS, HEAD_SIZE)
        value_slice_view = lax.dynamic_slice_in_dim(padded_values, row_beginning, slice_view, 0).astype(jnp.float32).reshape(slice_view, KEY_VALUE_HEADS, HEAD_SIZE)
        query_seg = lax.dynamic_slice_in_dim(segment.astype(jnp.int32), row_beginning, CONTEXT_TOKENS, 0)
        key_seg = lax.dynamic_slice_in_dim(seg_pad, row_beginning, slice_view, 0)
        query_pos = row_beginning + jnp.arange(CONTEXT_TOKENS, dtype=jnp.int32)
        key_pos = row_beginning - pad_amount + jnp.arange(slice_view, dtype=jnp.int32)
        allowed = (query_seg[:, None] == key_seg[None, :]) & (key_pos[None, :] <= query_pos[:, None])
        scores = jnp.einsum('tkgd,skd->kgts', query_tile_rows, key_slice_view) * factor
        scores = jnp.where(allowed, scores, -jnp.inf)
        row_max = lax.optimization_barrier(jnp.max(scores, -1, keepdims=True))
        row_total = lax.optimization_barrier(jnp.sum(jnp.exp(scores - row_max), -1, keepdims=True))
        log_total = row_max + jnp.log(row_total)
        weights = jnp.where(allowed, jnp.exp(scores - log_total), 0.0)
        weights_low = rounded(weights)
        attended = jnp.einsum('kgts,skd->tkgd', weights_low, value_slice_view).astype(jnp.bfloat16)
        delta_row = lax.optimization_barrier(jnp.sum(block_gradients * attended.astype(jnp.float32), -1))
        d_weights = jnp.einsum('tkgd,skd->kgts', block_gradients, value_slice_view)
        d_scores = weights * (d_weights - jnp.transpose(delta_row, (1, 2, 0))[..., None])
        d_scores_low = rounded(d_scores)
        d_query = (jnp.einsum('kgts,skd->tkgd', d_scores_low, key_slice_view) * factor).astype(jnp.bfloat16)
        key_portion = jnp.einsum('kgts,tkgd->skd', d_scores_low, query_tile_rows) * factor
        value_portion = jnp.einsum('kgts,tkgd->skd', weights_low, block_gradients)
        previous_key = lax.dynamic_slice_in_dim(key_gradient, row_beginning, slice_view, 0)
        previous_value = lax.dynamic_slice_in_dim(value_gradient, row_beginning, slice_view, 0)
        key_gradient = lax.dynamic_update_slice_in_dim(key_gradient, previous_key + key_portion.reshape(slice_view, KEY_VALUE_HEADS * HEAD_SIZE), row_beginning, 0)
        value_gradient = lax.dynamic_update_slice_in_dim(value_gradient, previous_value + value_portion.reshape(slice_view, KEY_VALUE_HEADS * HEAD_SIZE), row_beginning, 0)
        return ((key_gradient, value_gradient), (attended.reshape(CONTEXT_TOKENS, QUERY_HEADS * HEAD_SIZE), d_query.reshape(CONTEXT_TOKENS, QUERY_HEADS * HEAD_SIZE)))
    empty_gradient = jnp.zeros((ROW_TOKENS + pad_amount, KEY_VALUE_HEADS * HEAD_SIZE), jnp.float32)
    (key_gradient, value_gradient), (attended, d_query) = lax.scan(one_block, (empty_gradient, empty_gradient), jnp.arange(block_count, dtype=jnp.int32))
    return (attended.reshape(ROW_TOKENS, QUERY_HEADS * HEAD_SIZE), d_query.reshape(ROW_TOKENS, QUERY_HEADS * HEAD_SIZE), key_gradient[pad_amount:].astype(jnp.bfloat16), value_gradient[pad_amount:].astype(jnp.bfloat16))
```

```python
import functools
import math

import jax
import jax.numpy as jnp
from jax import lax
from jax.experimental import pallas as pl
from jax.experimental.pallas import tpu as pltpu
from jax.sharding import PartitionSpec as P

QUERY_HEADS = 48
KEY_VALUE_HEADS = 8
HEAD_SIZE = 128
REACH = 2
GROUP = QUERY_HEADS // KEY_VALUE_HEADS
PAIR = 2
MESH = pl.DeviceIdType.MESH


def nt(a, b):
    return lax.dot_general(a, b, (((1,), (1,)), ((), ())), preferred_element_type=jnp.float32)


def tn(a, b):
    return lax.dot_general(a, b, (((0,), (0,)), ((), ())), preferred_element_type=jnp.float32)


def nn(a, b):
    return lax.dot_general(a, b, (((1,), (0,)), ((), ())), preferred_element_type=jnp.float32)


def kernel(
    inners, shards, heads,
    query_ref, key_ref, value_ref, cot_ref, seg_ref,
    att_ref, dq_ref, dk_ref, dv_ref,
    q_vm, do_vm, seg_vm, att_vm, dq_vm, kv, own, stage, got, final, bias, low,
    in_sem, seg_sem, out_sem, loc_sem,
    y_send, y_recv, f_send, f_recv, b_send, b_recv, z_send, z_recv, z_loc,
):
    D = HEAD_SIZE
    length = q_vm.shape[0]
    groups = kv.shape[3] // D
    width = groups * D
    part = length // heads
    qw = GROUP * D
    lanes = PAIR * D
    scale = 1.0 / math.sqrt(D)
    shard = lax.axis_index("outer") * inners + lax.axis_index("inner")
    me = lax.axis_index("head")

    def at_shard(target):
        return {"outer": lax.div(target, inners), "inner": lax.rem(target, inners), "head": me}

    def at_head(target):
        return {"head": target}

    def rows(p):
        return pl.ds(pl.multiple_of(p * part, part), part)

    def cols(start, size):
        return pl.ds(pl.multiple_of(start, D), size)

    def before(j):
        return lax.rem(me + heads - j, heads)

    def after(j):
        return lax.rem(me + j, heads)

    both = (key_ref, value_ref)
    outs = (dk_ref, dv_ref)

    def load(g, which):
        src, dst = ((query_ref, q_vm), (cot_ref, do_vm))[which]
        c = cols(g * qw, qw)
        return pltpu.make_async_copy(src.at[:, c], dst.at[:, c], in_sem.at[which, g])

    def save(g, which):
        src, dst = ((att_vm, att_ref), (dq_vm, dq_ref))[which]
        c = cols(g * qw, qw)
        return pltpu.make_async_copy(src.at[:, c], dst.at[:, c], out_sem.at[which, g])

    def local(g, t):
        return pltpu.make_async_copy(
            both[t].at[:, cols(me * width + g * D, D)],
            kv.at[0, t, rows(me), cols(g * D, D)],
            loc_sem.at[t, g],
        )

    def across(g, t, j):
        return pltpu.make_async_remote_copy(
            src_ref=both[t].at[:, cols(after(j) * width + g * D, D)],
            dst_ref=kv.at[0, t, rows(me), cols(g * D, D)],
            send_sem=y_send.at[j - 1, t, g],
            recv_sem=y_recv.at[j - 1, t, g],
            device_id=at_head(after(j)),
            device_id_type=MESH,
        )

    def onward(g, t, j, o):
        r = rows(before(j))
        if j == 0:
            src = both[t].at[:, cols(me * width + g * D, D)]
        else:
            src = kv.at[0, t, r, cols(g * D, D)]
        return pltpu.make_async_remote_copy(
            src_ref=src,
            dst_ref=kv.at[o, t, r, cols(g * D, D)],
            send_sem=f_send.at[o - 1, j, t, g],
            recv_sem=f_recv.at[o - 1, j, t, g],
            device_id=at_shard(shard + o),
            device_id_type=MESH,
        )

    def back(g, t, o):
        return pltpu.make_async_remote_copy(
            src_ref=stage.at[o - 1, t, :, cols(g * D, D)],
            dst_ref=got.at[o - 1, t, :, cols(g * D, D)],
            send_sem=b_send.at[o - 1, t, g],
            recv_sem=b_recv.at[o - 1, t, g],
            device_id=at_shard(shard - o),
            device_id_type=MESH,
        )

    def home(g, t, j):
        return pltpu.make_async_remote_copy(
            src_ref=final.at[t, rows(after(j)), cols(g * D, D)],
            dst_ref=outs[t].at[:, cols(me * width + g * D, D)],
            send_sem=z_send.at[j - 1, t, g],
            recv_sem=z_recv.at[j - 1, t, g],
            device_id=at_head(after(j)),
            device_id_type=MESH,
        )

    def stay(g, t):
        return pltpu.make_async_copy(
            final.at[t, rows(me), cols(g * D, D)],
            outs[t].at[:, cols(me * width + g * D, D)],
            z_loc.at[t, g],
        )

    has_next = [None] + [shard + o < shards for o in range(1, REACH + 1)]
    has_prev = [None] + [shard >= o for o in range(1, REACH + 1)]

    barrier = pltpu.get_barrier_semaphore()
    for j in range(1, heads):
        pl.semaphore_signal(barrier, inc=1, device_id=at_head(after(j)), device_id_type=MESH)
    for o in range(1, REACH + 1):
        @pl.when(has_next[o])
        def _():
            pl.semaphore_signal(barrier, inc=1, device_id=at_shard(shard + o), device_id_type=MESH)

        @pl.when(has_prev[o])
        def _():
            pl.semaphore_signal(barrier, inc=1, device_id=at_shard(shard - o), device_id_type=MESH)

    seg_copy = pltpu.make_async_copy(seg_ref, seg_vm, seg_sem)
    seg_copy.start()
    for g in range(groups):
        for t in range(2):
            local(g, t).start()
            load(g, t).start()

    for o in range(1, REACH + 1):
        @pl.when(jnp.logical_not(has_prev[o]))
        def _():
            kv[o] = jnp.zeros(kv.shape[1:], kv.dtype)

        @pl.when(jnp.logical_not(has_next[o]))
        def _():
            got[o - 1] = jnp.zeros(got.shape[1:], got.dtype)

    partners = heads - 1
    for o in range(1, REACH + 1):
        partners = partners + jnp.where(has_next[o], 1, 0) + jnp.where(has_prev[o], 1, 0)
    pl.semaphore_wait(barrier, partners)

    for g in range(groups):
        for t in range(2):
            for j in range(1, heads):
                across(g, t, j).start()
        for o in range(1, REACH + 1):
            @pl.when(has_next[o])
            def _():
                for t in range(2):
                    onward(g, t, 0, o).start()

    seg_copy.wait()

    def seg_row(o):
        row = seg_vm[pl.ds(jnp.maximum(shard - o, 0), 1), :]
        return jnp.where(shard >= o, row, -1)

    def tall(row):
        return jnp.transpose(jnp.broadcast_to(row, (length, length)))

    seg_here = seg_row(0)
    key_index = lax.broadcasted_iota(jnp.int32, (length, length), 0)
    query_index = lax.broadcasted_iota(jnp.int32, (length, length), 1)
    lower = key_index <= query_index
    merged = jnp.where(lower, tall(seg_here), tall(seg_row(2)))
    blocked = -jnp.inf
    bias_own = jnp.where(merged == seg_here, 0.0, blocked)
    bias_prev = jnp.where(tall(seg_row(1)) == seg_here, 0.0, blocked)
    one_low = jnp.where(lower, 1.0, 0.0).astype(jnp.bfloat16)
    for i in range(PAIR):
        bias[0, :, i * D:(i + 1) * D] = bias_own
        bias[1, :, i * D:(i + 1) * D] = bias_prev
        low[:, i * D:(i + 1) * D] = one_low

    for g in range(groups):
        for j in range(1, heads):
            for t in range(2):
                across(g, t, j).wait_recv()
            for o in range(1, REACH + 1):
                @pl.when(has_next[o])
                def _():
                    for t in range(2):
                        onward(g, t, j, o).start()

    wide_lower = lax.broadcasted_iota(jnp.int32, (length, lanes), 0) <= lax.rem(
        lax.broadcasted_iota(jnp.int32, (length, lanes), 1), D
    )

    def one_group(g, carry):
        for t in range(2):
            local(g, t).wait()
            load(g, t).wait()
        for o in range(1, REACH + 1):
            @pl.when(has_prev[o])
            def _():
                for j in range(heads):
                    for t in range(2):
                        onward(g, t, j, o).wait_recv()
        c = cols(g * D, D)
        order = (0, 2, 1)
        keys = jnp.concatenate([kv[o, 0, :, c] for o in order], 0)
        values = jnp.concatenate([kv[o, 1, :, c] for o in order], 0)
        dk_sum = None
        for u in range(GROUP // PAIR):
            first = g * qw + u * lanes
            spans = [cols(first + i * D, D) for i in range(PAIR)]
            q = jnp.concatenate([q_vm[:, s] for s in spans], 0)
            do = jnp.concatenate([do_vm[:, s] for s in spans], 0)
            scores = nt(keys, q)
            d_w = nt(values, do)
            s_own = jnp.where(wide_lower, scores[:length], scores[length:2 * length]) + bias[0]
            s_prev = scores[2 * length:] + bias[1]
            top = jnp.maximum(
                jnp.max(s_own, 0, keepdims=True), jnp.max(s_prev, 0, keepdims=True)
            )
            unit = scale * math.log2(math.e)
            e_own = jnp.exp2((s_own - top) * unit)
            e_prev = jnp.exp2((s_prev - top) * unit)
            inv = 1.0 / (
                jnp.sum(e_own, 0, keepdims=True) + jnp.sum(e_prev, 0, keepdims=True)
            )
            w_own = e_own * inv
            w_prev = e_prev * inv
            r_own = w_own.astype(jnp.bfloat16)
            r_prev = w_prev.astype(jnp.bfloat16)
            d_own = jnp.where(wide_lower, d_w[:length], d_w[length:2 * length])
            d_prev = d_w[2 * length:]
            delta = jnp.sum(r_own.astype(jnp.float32) * d_own, 0, keepdims=True) + jnp.sum(
                r_prev.astype(jnp.float32) * d_prev, 0, keepdims=True
            )
            g_own = (w_own * (d_own - delta)).astype(jnp.bfloat16)
            g_prev = (w_prev * (d_prev - delta)).astype(jnp.bfloat16)
            keep = low[...]
            r_low = r_own * keep
            g_low = g_own * keep
            weights = jnp.concatenate([r_low, r_own - r_low, r_prev], 0)
            d_scores = jnp.concatenate([g_low, g_own - g_low, g_prev], 0)
            att = jnp.transpose(tn(values, weights))
            dq = jnp.transpose(tn(keys, d_scores) * scale)
            for i, s in enumerate(spans):
                att_vm[:, s] = att[i * length:(i + 1) * length].astype(jnp.bfloat16)
                dq_vm[:, s] = dq[i * length:(i + 1) * length].astype(jnp.bfloat16)
            dk_part = nn(d_scores, q)
            dv_part = nn(weights, do)
            dk_sum = dk_part if dk_sum is None else dk_sum + dk_part
            dv_sum = dv_part if u == 0 else dv_sum + dv_part
        for t, total in enumerate((dk_sum * scale, dv_sum)):
            for at, o in enumerate(order):
                block = total[at * length:(at + 1) * length]
                if o == 0:
                    own[t, :, c] = block
                else:
                    stage[o - 1, t, :, c] = block.astype(jnp.bfloat16)
        for o in range(REACH, 0, -1):
            @pl.when(has_prev[o])
            def _():
                for t in range(2):
                    back(g, t, o).start()
        for t in range(2):
            save(g, t).start()
        return carry

    lax.fori_loop(0, groups, one_group, 0)

    for g in range(groups):
        c = cols(g * D, D)
        for o in range(1, REACH + 1):
            @pl.when(has_next[o])
            def _():
                for t in range(2):
                    back(g, t, o).wait_recv()
        for t in range(2):
            total = own[t, :, c]
            for o in range(1, REACH + 1):
                total = total + got[o - 1, t, :, c].astype(jnp.float32)
            final[t, :, c] = total.astype(jnp.bfloat16)
            for j in range(1, heads):
                home(g, t, j).start()
            stay(g, t).start()

    for g in range(groups):
        for t in range(2):
            save(g, t).wait()
            stay(g, t).wait()
            for j in range(1, heads):
                across(g, t, j).wait_send()
                home(g, t, j).wait()
        for o in range(1, REACH + 1):
            @pl.when(has_next[o])
            def _():
                for j in range(heads):
                    for t in range(2):
                        onward(g, t, j, o).wait_send()

            @pl.when(has_prev[o])
            def _():
                for t in range(2):
                    back(g, t, o).wait_send()


def body(mesh, query, key, value, output_cotangent, segment):
    length, wide = query.shape
    part, kv_wide = key.shape
    heads = mesh.shape["head"]
    inners = mesh.shape["inner"]
    shards = mesh.shape["outer"] * inners
    groups = kv_wide // heads // HEAD_SIZE
    width = groups * HEAD_SIZE
    bf, f32 = jnp.bfloat16, jnp.float32
    dma = pltpu.SemaphoreType.DMA
    peers = max(heads - 1, 1)
    lanes = PAIR * HEAD_SIZE
    return pl.pallas_call(
        functools.partial(kernel, inners, shards, heads),
        out_shape=(
            jax.ShapeDtypeStruct((length, wide), bf),
            jax.ShapeDtypeStruct((length, wide), bf),
            jax.ShapeDtypeStruct((part, kv_wide), bf),
            jax.ShapeDtypeStruct((part, kv_wide), bf),
        ),
        in_specs=[pl.BlockSpec(memory_space=pl.ANY)] * 5,
        out_specs=[pl.BlockSpec(memory_space=pl.ANY)] * 4,
        scratch_shapes=[
            pltpu.VMEM((length, wide), bf),
            pltpu.VMEM((length, wide), bf),
            pltpu.VMEM((shards, length), jnp.int32),
            pltpu.VMEM((length, wide), bf),
            pltpu.VMEM((length, wide), bf),
            pltpu.VMEM((REACH + 1, 2, length, width), bf),
            pltpu.VMEM((2, length, width), f32),
            pltpu.VMEM((REACH, 2, length, width), bf),
            pltpu.VMEM((REACH, 2, length, width), bf),
            pltpu.VMEM((2, length, width), bf),
            pltpu.VMEM((2, length, lanes), f32),
            pltpu.VMEM((length, lanes), bf),
            dma((2, groups)),
            dma(()),
            dma((2, groups)),
            dma((2, groups)),
            dma((peers, 2, groups)),
            dma((peers, 2, groups)),
            dma((REACH, heads, 2, groups)),
            dma((REACH, heads, 2, groups)),
            dma((REACH, 2, groups)),
            dma((REACH, 2, groups)),
            dma((peers, 2, groups)),
            dma((peers, 2, groups)),
            dma((2, groups)),
        ],
        compiler_params=pltpu.CompilerParams(
            collective_id=0, has_side_effects=True, vmem_limit_bytes=60 * 2**20
        ),
        name="packed_attention",
    )(query, key, value, output_cotangent, segment.reshape(shards, length))


def solution(mesh):
    in_specs = (
        P(("outer", "inner"), "head"),
        P(("outer", "inner", "head"), None),
        P(("outer", "inner", "head"), None),
        P(("outer", "inner"), "head"),
        P(),
    )
    out_specs = (
        P(("outer", "inner"), "head"),
        P(("outer", "inner"), "head"),
        P(("outer", "inner", "head"), None),
        P(("outer", "inner", "head"), None),
    )
    return jax.shard_map(
        functools.partial(body, mesh),
        mesh=mesh, in_specs=in_specs, out_specs=out_specs, check_vma=False,
    )
```

```python
import functools
import math

import jax
import jax.numpy as jnp
from jax import lax
from jax.experimental import pallas as pl
from jax.experimental.pallas import tpu as pltpu
from jax.sharding import PartitionSpec as P

QUERY_HEADS = 48
KEY_VALUE_HEADS = 8
HEAD_SIZE = 128
REACH = 2
GROUP = QUERY_HEADS // KEY_VALUE_HEADS
PAIR = 2
MESH = pl.DeviceIdType.MESH


def nt(a, b):
    return lax.dot_general(a, b, (((1,), (1,)), ((), ())), preferred_element_type=jnp.float32)


def tn(a, b):
    return lax.dot_general(a, b, (((0,), (0,)), ((), ())), preferred_element_type=jnp.float32)


def nn(a, b):
    return lax.dot_general(a, b, (((1,), (0,)), ((), ())), preferred_element_type=jnp.float32)


def kernel(
    inners, shards, heads,
    query_ref, key_ref, value_ref, cot_ref, seg_ref,
    att_ref, dq_ref, dk_ref, dv_ref,
    q_vm, do_vm, seg_vm, kv, own, hold, mid, stage, got, final, bias, low,
    in_sem, seg_sem, loc_sem,
    y_send, y_recv, f_send, f_recv, r_send, m_recv, b_send, b_recv, z_send, z_recv, z_loc,
):
    D = HEAD_SIZE
    length = q_vm.shape[0]
    groups = kv.shape[3] // D
    width = groups * D
    part = length // heads
    qw = GROUP * D
    lanes = PAIR * D
    scale = 1.0 / math.sqrt(D)
    shard = lax.axis_index("outer") * inners + lax.axis_index("inner")
    me = lax.axis_index("head")

    def at_shard(target):
        return {"outer": lax.div(target, inners), "inner": lax.rem(target, inners), "head": me}

    def at_head(target):
        return {"head": target}

    def rows(p):
        return pl.ds(pl.multiple_of(p * part, part), part)

    def cols(start, size):
        return pl.ds(pl.multiple_of(start, D), size)

    def before(j):
        return lax.rem(me + heads - j, heads)

    def after(j):
        return lax.rem(me + j, heads)

    both = (key_ref, value_ref)
    outs = (dk_ref, dv_ref)

    def load(g, which):
        src, dst = ((query_ref, q_vm), (cot_ref, do_vm))[which]
        c = cols(g * qw, qw)
        return pltpu.make_async_copy(src.at[:, c], dst.at[:, c], in_sem.at[which, g])

    def local(g, t):
        return pltpu.make_async_copy(
            both[t].at[:, cols(me * width + g * D, D)],
            kv.at[0, t, rows(me), cols(g * D, D)],
            loc_sem.at[t, g],
        )

    def across(g, t, j):
        return pltpu.make_async_remote_copy(
            src_ref=both[t].at[:, cols(after(j) * width + g * D, D)],
            dst_ref=kv.at[0, t, rows(me), cols(g * D, D)],
            send_sem=y_send.at[j - 1, t, g],
            recv_sem=y_recv.at[j - 1, t, g],
            device_id=at_head(after(j)),
            device_id_type=MESH,
        )

    def onward(g, t, j, o):
        r = rows(before(j))
        if j == 0:
            src = both[t].at[:, cols(me * width + g * D, D)]
        else:
            src = kv.at[0, t, r, cols(g * D, D)]
        return pltpu.make_async_remote_copy(
            src_ref=src,
            dst_ref=kv.at[o, t, r, cols(g * D, D)],
            send_sem=f_send.at[o - 1, j, t, g],
            recv_sem=f_recv.at[o - 1, j, t, g],
            device_id=at_shard(shard + o),
            device_id_type=MESH,
        )

    def relay(g, t, j):
        r = rows(before(j))
        return pltpu.make_async_remote_copy(
            src_ref=kv.at[1, t, r, cols(g * D, D)],
            dst_ref=kv.at[2, t, r, cols(g * D, D)],
            send_sem=r_send.at[j, t, g],
            recv_sem=f_recv.at[1, j, t, g],
            device_id=at_shard(shard + 1),
            device_id_type=MESH,
        )

    def back_near(g, t):
        return pltpu.make_async_remote_copy(
            src_ref=stage.at[1, t, :, cols(g * D, D)],
            dst_ref=mid.at[t, :, cols(g * D, D)],
            send_sem=b_send.at[1, t, g],
            recv_sem=m_recv.at[t, g],
            device_id=at_shard(shard - 1),
            device_id_type=MESH,
        )

    def back(g, t, o):
        return pltpu.make_async_remote_copy(
            src_ref=stage.at[o - 1, t, :, cols(g * D, D)],
            dst_ref=got.at[o - 1, t, :, cols(g * D, D)],
            send_sem=b_send.at[o - 1, t, g],
            recv_sem=b_recv.at[o - 1, t, g],
            device_id=at_shard(shard - o),
            device_id_type=MESH,
        )

    def home(g, t, j):
        return pltpu.make_async_remote_copy(
            src_ref=final.at[t, rows(after(j)), cols(g * D, D)],
            dst_ref=outs[t].at[:, cols(me * width + g * D, D)],
            send_sem=z_send.at[j - 1, t, g],
            recv_sem=z_recv.at[j - 1, t, g],
            device_id=at_head(after(j)),
            device_id_type=MESH,
        )

    def stay(g, t):
        return pltpu.make_async_copy(
            final.at[t, rows(me), cols(g * D, D)],
            outs[t].at[:, cols(me * width + g * D, D)],
            z_loc.at[t, g],
        )

    has_next = [None] + [shard + o < shards for o in range(1, REACH + 1)]
    has_prev = [None] + [shard >= o for o in range(1, REACH + 1)]

    even = lax.rem(shard, 2) == 0
    odd = jnp.logical_not(even)
    deals_next = [None, has_next[1], jnp.logical_and(even, has_next[2])]
    deals_prev = [None, has_prev[1], jnp.logical_and(even, has_prev[2])]
    relays = deals_prev[2]

    barrier = pltpu.get_barrier_semaphore()
    for j in range(1, heads):
        pl.semaphore_signal(barrier, inc=1, device_id=at_head(after(j)), device_id_type=MESH)
    for o in range(1, REACH + 1):
        @pl.when(deals_next[o])
        def _():
            pl.semaphore_signal(barrier, inc=1, device_id=at_shard(shard + o), device_id_type=MESH)

        @pl.when(deals_prev[o])
        def _():
            pl.semaphore_signal(barrier, inc=1, device_id=at_shard(shard - o), device_id_type=MESH)

    seg_copy = pltpu.make_async_copy(seg_ref, seg_vm, seg_sem)
    seg_copy.start()
    for g in range(groups):
        for t in range(2):
            local(g, t).start()
            load(g, t).start()

    for o in range(1, REACH + 1):
        @pl.when(jnp.logical_not(has_prev[o]))
        def _():
            kv[o] = jnp.zeros(kv.shape[1:], kv.dtype)

        @pl.when(jnp.logical_not(deals_next[o]))
        def _():
            got[o - 1] = jnp.zeros(got.shape[1:], got.dtype)

    partners = heads - 1
    for o in range(1, REACH + 1):
        partners = partners + jnp.where(deals_next[o], 1, 0) + jnp.where(deals_prev[o], 1, 0)
    pl.semaphore_wait(barrier, partners)

    for g in range(groups):
        for t in range(2):
            for j in range(1, heads):
                across(g, t, j).start()
        for o in range(REACH, 0, -1):
            @pl.when(deals_next[o])
            def _():
                for t in range(2):
                    onward(g, t, 0, o).start()

    seg_copy.wait()

    def seg_row(o):
        row = seg_vm[pl.ds(jnp.maximum(shard - o, 0), 1), :]
        return jnp.where(shard >= o, row, -1)

    def tall(row):
        return jnp.transpose(jnp.broadcast_to(row, (length, length)))

    seg_here = seg_row(0)
    key_index = lax.broadcasted_iota(jnp.int32, (length, length), 0)
    query_index = lax.broadcasted_iota(jnp.int32, (length, length), 1)
    lower = key_index <= query_index
    merged = jnp.where(lower, tall(seg_here), tall(seg_row(2)))
    blocked = -jnp.inf
    bias_own = jnp.where(merged == seg_here, 0.0, blocked)
    bias_prev = jnp.where(tall(seg_row(1)) == seg_here, 0.0, blocked)
    one_low = jnp.where(lower, 1.0, 0.0).astype(jnp.bfloat16)
    for i in range(PAIR):
        bias[0, :, i * D:(i + 1) * D] = bias_own
        bias[1, :, i * D:(i + 1) * D] = bias_prev
        low[:, i * D:(i + 1) * D] = one_low

    for g in range(groups):
        for j in range(1, heads):
            for t in range(2):
                across(g, t, j).wait_recv()
            for o in range(REACH, 0, -1):
                @pl.when(deals_next[o])
                def _():
                    for t in range(2):
                        onward(g, t, j, o).start()

    wide_lower = lax.broadcasted_iota(jnp.int32, (length, lanes), 0) <= lax.rem(
        lax.broadcasted_iota(jnp.int32, (length, lanes), 1), D
    )

    def merge(g):
        c = cols(g * D, D)
        for t in range(2):
            back_near(g, t).wait_recv()
            stage[0, t, :, c] = (hold[t, :, c] + mid[t, :, c].astype(jnp.float32)).astype(
                jnp.bfloat16
            )
            back(g, t, 1).start()

    def one_group(g, carry):
        for t in range(2):
            local(g, t).wait()
            load(g, t).wait()
        for o in range(1, REACH + 1):
            @pl.when(has_prev[o])
            def _():
                for j in range(heads):
                    for t in range(2):
                        onward(g, t, j, o).wait_recv()

            if o == 1:
                @pl.when(relays)
                def _():
                    for j in range(heads):
                        for t in range(2):
                            relay(g, t, j).start()
        c = cols(g * D, D)
        order = (0, 2, 1)
        keys = jnp.concatenate([kv[o, 0, :, c] for o in order], 0)
        values = jnp.concatenate([kv[o, 1, :, c] for o in order], 0)
        dk_sum = None
        for u in range(GROUP // PAIR):
            first = g * qw + u * lanes
            spans = [cols(first + i * D, D) for i in range(PAIR)]
            q = jnp.concatenate([q_vm[:, s] for s in spans], 0)
            do = jnp.concatenate([do_vm[:, s] for s in spans], 0)
            scores = nt(keys, q)
            d_w = nt(values, do)
            s_own = jnp.where(wide_lower, scores[:length], scores[length:2 * length]) + bias[0]
            s_prev = scores[2 * length:] + bias[1]
            top = jnp.maximum(
                jnp.max(s_own, 0, keepdims=True), jnp.max(s_prev, 0, keepdims=True)
            )
            unit = scale * math.log2(math.e)
            e_own = jnp.exp2((s_own - top) * unit)
            e_prev = jnp.exp2((s_prev - top) * unit)
            inv = 1.0 / (
                jnp.sum(e_own, 0, keepdims=True) + jnp.sum(e_prev, 0, keepdims=True)
            )
            w_own = e_own * inv
            w_prev = e_prev * inv
            r_own = w_own.astype(jnp.bfloat16)
            r_prev = w_prev.astype(jnp.bfloat16)
            d_own = jnp.where(wide_lower, d_w[:length], d_w[length:2 * length])
            d_prev = d_w[2 * length:]
            delta = jnp.sum(r_own.astype(jnp.float32) * d_own, 0, keepdims=True) + jnp.sum(
                r_prev.astype(jnp.float32) * d_prev, 0, keepdims=True
            )
            g_own = (w_own * (d_own - delta)).astype(jnp.bfloat16)
            g_prev = (w_prev * (d_prev - delta)).astype(jnp.bfloat16)
            keep = low[...]
            r_low = r_own * keep
            g_low = g_own * keep
            weights = jnp.concatenate([r_low, r_own - r_low, r_prev], 0)
            d_scores = jnp.concatenate([g_low, g_own - g_low, g_prev], 0)
            att = jnp.transpose(tn(values, weights))
            dq = jnp.transpose(tn(keys, d_scores) * scale)
            for i, s in enumerate(spans):
                att_ref[:, s] = att[i * length:(i + 1) * length].astype(jnp.bfloat16)
                dq_ref[:, s] = dq[i * length:(i + 1) * length].astype(jnp.bfloat16)
            dk_part = nn(d_scores, q)
            dv_part = nn(weights, do)
            dk_sum = dk_part if dk_sum is None else dk_sum + dk_part
            dv_sum = dv_part if u == 0 else dv_sum + dv_part
        for t, total in enumerate((dk_sum * scale, dv_sum)):
            for at, o in enumerate(order):
                block = total[at * length:(at + 1) * length]
                if o == 0:
                    own[t, :, c] = block
                elif o == 1:
                    hold[t, :, c] = block
                else:
                    stage[1, t, :, c] = block.astype(jnp.bfloat16)

        @pl.when(relays)
        def _():
            for t in range(2):
                back(g, t, 2).start()

            @pl.when(g >= 1)
            def _():
                merge(g - 1)

        @pl.when(jnp.logical_and(odd, has_prev[2]))
        def _():
            for t in range(2):
                back_near(g, t).start()

        @pl.when(odd)
        def _():
            for t in range(2):
                stage[0, t, :, c] = hold[t, :, c].astype(jnp.bfloat16)
                back(g, t, 1).start()
        return carry

    lax.fori_loop(0, groups, one_group, 0)

    @pl.when(relays)
    def _():
        merge(groups - 1)

    for g in range(groups):
        c = cols(g * D, D)
        for o in range(1, REACH + 1):
            @pl.when(deals_next[o])
            def _():
                for t in range(2):
                    back(g, t, o).wait_recv()
        for t in range(2):
            total = own[t, :, c]
            for o in range(1, REACH + 1):
                total = total + got[o - 1, t, :, c].astype(jnp.float32)
            final[t, :, c] = total.astype(jnp.bfloat16)
            for j in range(1, heads):
                home(g, t, j).start()
            stay(g, t).start()

    for g in range(groups):
        for t in range(2):
            stay(g, t).wait()
            for j in range(1, heads):
                across(g, t, j).wait_send()
                home(g, t, j).wait()
        for o in range(1, REACH + 1):
            @pl.when(deals_next[o])
            def _():
                for j in range(heads):
                    for t in range(2):
                        onward(g, t, j, o).wait_send()

            @pl.when(has_prev[o])
            def _():
                for t in range(2):
                    back(g, t, o).wait_send()

        @pl.when(relays)
        def _():
            for j in range(heads):
                for t in range(2):
                    relay(g, t, j).wait_send()


def write_out(*refs):
    count = len(refs) // 2
    sems = refs[-1]
    copies = []
    for i in range(count):
        src, dst = refs[i], refs[count + i]
        half = src.shape[0] // 2
        for k in range(2):
            r = pl.ds(k * half, half)
            copies.append(pltpu.make_async_copy(src.at[r], dst.at[r], sems.at[i, k]))
    for copy in copies:
        copy.start()
    for copy in copies:
        copy.wait()


def body(mesh, query, key, value, output_cotangent, segment):
    length, wide = query.shape
    part, kv_wide = key.shape
    heads = mesh.shape["head"]
    inners = mesh.shape["inner"]
    shards = mesh.shape["outer"] * inners
    groups = kv_wide // heads // HEAD_SIZE
    width = groups * HEAD_SIZE
    bf, f32 = jnp.bfloat16, jnp.float32
    dma = pltpu.SemaphoreType.DMA
    peers = max(heads - 1, 1)
    lanes = PAIR * HEAD_SIZE
    shapes = ((length, wide), (length, wide), (part, kv_wide), (part, kv_wide))
    results = pl.pallas_call(
        functools.partial(kernel, inners, shards, heads),
        out_shape=tuple(pltpu.VMEM(shape, bf) for shape in shapes),
        in_specs=[pl.BlockSpec(memory_space=pltpu.HBM)] * 5,
        out_specs=[pl.BlockSpec(memory_space=pltpu.VMEM)] * 4,
        scratch_shapes=[
            pltpu.VMEM((length, wide), bf),
            pltpu.VMEM((length, wide), bf),
            pltpu.VMEM((shards, length), jnp.int32),
            pltpu.VMEM((REACH + 1, 2, length, width), bf),
            pltpu.VMEM((2, length, width), f32),
            pltpu.VMEM((2, length, width), f32),
            pltpu.VMEM((2, length, width), bf),
            pltpu.VMEM((REACH, 2, length, width), bf),
            pltpu.VMEM((REACH, 2, length, width), bf),
            pltpu.VMEM((2, length, width), bf),
            pltpu.VMEM((2, length, lanes), f32),
            pltpu.VMEM((length, lanes), bf),
            dma((2, groups)),
            dma(()),
            dma((2, groups)),
            dma((peers, 2, groups)),
            dma((peers, 2, groups)),
            dma((REACH, heads, 2, groups)),
            dma((REACH, heads, 2, groups)),
            dma((heads, 2, groups)),
            dma((2, groups)),
            dma((REACH, 2, groups)),
            dma((REACH, 2, groups)),
            dma((peers, 2, groups)),
            dma((peers, 2, groups)),
            dma((2, groups)),
        ],
        compiler_params=pltpu.CompilerParams(
            collective_id=0, has_side_effects=True, vmem_limit_bytes=61 * 2**20
        ),
        name="packed_attention",
    )(query, key, value, output_cotangent, segment.reshape(shards, length))
    return pl.pallas_call(
        write_out,
        out_shape=tuple(jax.ShapeDtypeStruct(shape, bf) for shape in shapes),
        in_specs=[pl.BlockSpec(memory_space=pltpu.VMEM)] * 4,
        out_specs=[pl.BlockSpec(memory_space=pltpu.HBM)] * 4,
        scratch_shapes=[dma((len(shapes), 2))],
        name="write_out",
    )(*results)


def solution(mesh):
    in_specs = (
        P(("outer", "inner"), "head"),
        P(("outer", "inner", "head"), None),
        P(("outer", "inner", "head"), None),
        P(("outer", "inner"), "head"),
        P(),
    )
    out_specs = (
        P(("outer", "inner"), "head"),
        P(("outer", "inner"), "head"),
        P(("outer", "inner", "head"), None),
        P(("outer", "inner", "head"), None),
    )
    return jax.shard_map(
        functools.partial(body, mesh),
        mesh=mesh, in_specs=in_specs, out_specs=out_specs, check_vma=False,
    )
```

```python
import functools
import math

import jax
import jax.numpy as jnp
from jax import lax
from jax.experimental import pallas as pl
from jax.experimental.pallas import tpu as pltpu
from jax.sharding import PartitionSpec as P

QUERY_HEADS = 48
KEY_VALUE_HEADS = 8
HEAD_SIZE = 128
REACH = 2
GROUP = QUERY_HEADS // KEY_VALUE_HEADS
PAIR = 2
MESH = pl.DeviceIdType.MESH


def nt(a, b):
    return lax.dot_general(a, b, (((1,), (1,)), ((), ())), preferred_element_type=jnp.float32)


def tn(a, b):
    return lax.dot_general(a, b, (((0,), (0,)), ((), ())), preferred_element_type=jnp.float32)


def nn(a, b):
    return lax.dot_general(a, b, (((1,), (0,)), ((), ())), preferred_element_type=jnp.float32)


def kernel(
    inners, shards, heads,
    query_ref, key_ref, value_ref, cot_ref, seg_ref,
    att_ref, dq_ref, dk_ref, dv_ref,
    q_vm, do_vm, seg_vm, kv, own, hold, mid, stage, got, final, bias, low, w_vm, ds_vm,
    in_sem, seg_sem, loc_sem,
    y_send, y_recv, f_send, f_recv, r_send, m_recv, b_send, b_recv, z_send, z_recv, z_loc,
):
    D = HEAD_SIZE
    length = q_vm.shape[0]
    groups = kv.shape[3] // D
    width = groups * D
    part = length // heads
    qw = GROUP * D
    lanes = PAIR * D
    scale = 1.0 / math.sqrt(D)
    shard = lax.axis_index("outer") * inners + lax.axis_index("inner")
    me = lax.axis_index("head")

    def at_shard(target):
        return {"outer": lax.div(target, inners), "inner": lax.rem(target, inners), "head": me}

    def at_head(target):
        return {"head": target}

    def rows(p):
        return pl.ds(pl.multiple_of(p * part, part), part)

    def cols(start, size):
        return pl.ds(pl.multiple_of(start, D), size)

    def before(j):
        return lax.rem(me + heads - j, heads)

    def after(j):
        return lax.rem(me + j, heads)

    both = (key_ref, value_ref)
    outs = (dk_ref, dv_ref)

    def load(g, which):
        src, dst = ((query_ref, q_vm), (cot_ref, do_vm))[which]
        c = cols(g * qw, qw)
        return pltpu.make_async_copy(src.at[:, c], dst.at[:, c], in_sem.at[which, g])

    def local(g, t):
        return pltpu.make_async_copy(
            both[t].at[:, cols(me * width + g * D, D)],
            kv.at[0, t, rows(me), cols(g * D, D)],
            loc_sem.at[t, g],
        )

    def across(g, t, j):
        return pltpu.make_async_remote_copy(
            src_ref=both[t].at[:, cols(after(j) * width + g * D, D)],
            dst_ref=kv.at[0, t, rows(me), cols(g * D, D)],
            send_sem=y_send.at[j - 1, t, g],
            recv_sem=y_recv.at[j - 1, t, g],
            device_id=at_head(after(j)),
            device_id_type=MESH,
        )

    def onward(g, t, j, o):
        r = rows(before(j))
        if j == 0:
            src = both[t].at[:, cols(me * width + g * D, D)]
        else:
            src = kv.at[0, t, r, cols(g * D, D)]
        return pltpu.make_async_remote_copy(
            src_ref=src,
            dst_ref=kv.at[o, t, r, cols(g * D, D)],
            send_sem=f_send.at[o - 1, j, t, g],
            recv_sem=f_recv.at[o - 1, j, t, g],
            device_id=at_shard(shard + o),
            device_id_type=MESH,
        )

    def relay(g, t, j):
        r = rows(before(j))
        return pltpu.make_async_remote_copy(
            src_ref=kv.at[1, t, r, cols(g * D, D)],
            dst_ref=kv.at[2, t, r, cols(g * D, D)],
            send_sem=r_send.at[j, t, g],
            recv_sem=f_recv.at[1, j, t, g],
            device_id=at_shard(shard + 1),
            device_id_type=MESH,
        )

    def back_near(g, t):
        return pltpu.make_async_remote_copy(
            src_ref=stage.at[1, t, :, cols(g * D, D)],
            dst_ref=mid.at[t, :, cols(g * D, D)],
            send_sem=b_send.at[1, t, g],
            recv_sem=m_recv.at[t, g],
            device_id=at_shard(shard - 1),
            device_id_type=MESH,
        )

    def back(g, t, o):
        return pltpu.make_async_remote_copy(
            src_ref=stage.at[o - 1, t, :, cols(g * D, D)],
            dst_ref=got.at[o - 1, t, :, cols(g * D, D)],
            send_sem=b_send.at[o - 1, t, g],
            recv_sem=b_recv.at[o - 1, t, g],
            device_id=at_shard(shard - o),
            device_id_type=MESH,
        )

    def home(g, t, j):
        return pltpu.make_async_remote_copy(
            src_ref=final.at[t, rows(after(j)), cols(g * D, D)],
            dst_ref=outs[t].at[:, cols(me * width + g * D, D)],
            send_sem=z_send.at[j - 1, t, g],
            recv_sem=z_recv.at[j - 1, t, g],
            device_id=at_head(after(j)),
            device_id_type=MESH,
        )

    def stay(g, t):
        return pltpu.make_async_copy(
            final.at[t, rows(me), cols(g * D, D)],
            outs[t].at[:, cols(me * width + g * D, D)],
            z_loc.at[t, g],
        )

    has_next = [None] + [shard + o < shards for o in range(1, REACH + 1)]
    has_prev = [None] + [shard >= o for o in range(1, REACH + 1)]

    even = lax.rem(shard, 2) == 0
    odd = jnp.logical_not(even)
    deals_next = [None, has_next[1], jnp.logical_and(even, has_next[2])]
    deals_prev = [None, has_prev[1], jnp.logical_and(even, has_prev[2])]
    relays = deals_prev[2]

    barrier = pltpu.get_barrier_semaphore()
    for j in range(1, heads):
        pl.semaphore_signal(barrier, inc=1, device_id=at_head(after(j)), device_id_type=MESH)
    for o in range(1, REACH + 1):
        @pl.when(deals_next[o])
        def _():
            pl.semaphore_signal(barrier, inc=1, device_id=at_shard(shard + o), device_id_type=MESH)

        @pl.when(deals_prev[o])
        def _():
            pl.semaphore_signal(barrier, inc=1, device_id=at_shard(shard - o), device_id_type=MESH)

    seg_copy = pltpu.make_async_copy(seg_ref, seg_vm, seg_sem)
    seg_copy.start()
    for g in range(groups):
        for t in range(2):
            local(g, t).start()
            load(g, t).start()

    for o in range(1, REACH + 1):
        @pl.when(jnp.logical_not(has_prev[o]))
        def _():
            kv[o] = jnp.zeros(kv.shape[1:], kv.dtype)

        @pl.when(jnp.logical_not(deals_next[o]))
        def _():
            got[o - 1] = jnp.zeros(got.shape[1:], got.dtype)

    partners = heads - 1
    for o in range(1, REACH + 1):
        partners = partners + jnp.where(deals_next[o], 1, 0) + jnp.where(deals_prev[o], 1, 0)
    pl.semaphore_wait(barrier, partners)

    for g in range(groups):
        for t in range(2):
            for j in range(1, heads):
                across(g, t, j).start()
        for o in range(REACH, 0, -1):
            @pl.when(deals_next[o])
            def _():
                for t in range(2):
                    onward(g, t, 0, o).start()

    seg_copy.wait()

    def seg_row(o):
        row = seg_vm[pl.ds(jnp.maximum(shard - o, 0), 1), :]
        return jnp.where(shard >= o, row, -1)

    def tall(row):
        return jnp.transpose(jnp.broadcast_to(row, (length, length)))

    seg_here = seg_row(0)
    key_index = lax.broadcasted_iota(jnp.int32, (length, length), 0)
    query_index = lax.broadcasted_iota(jnp.int32, (length, length), 1)
    lower = key_index <= query_index
    merged = jnp.where(lower, tall(seg_here), tall(seg_row(2)))
    blocked = -jnp.inf
    bias_own = jnp.where(merged == seg_here, 0.0, blocked)
    bias_prev = jnp.where(tall(seg_row(1)) == seg_here, 0.0, blocked)
    one_low = jnp.where(lower, 1.0, 0.0).astype(jnp.bfloat16)
    for i in range(PAIR):
        bias[0, :, i * D:(i + 1) * D] = bias_own
        bias[1, :, i * D:(i + 1) * D] = bias_prev
        low[:, i * D:(i + 1) * D] = one_low

    for g in range(groups):
        for j in range(1, heads):
            for t in range(2):
                across(g, t, j).wait_recv()
            for o in range(REACH, 0, -1):
                @pl.when(deals_next[o])
                def _():
                    for t in range(2):
                        onward(g, t, j, o).start()

    wide_lower = lax.broadcasted_iota(jnp.int32, (length, lanes), 0) <= lax.rem(
        lax.broadcasted_iota(jnp.int32, (length, lanes), 1), D
    )

    order = (0, 2, 1)

    def merge(g):
        c = cols(g * D, D)
        for t in range(2):
            back_near(g, t).wait_recv()
            stage[0, t, :, c] = (hold[t, :, c] + mid[t, :, c].astype(jnp.float32)).astype(
                jnp.bfloat16
            )
            back(g, t, 1).start()

    def one_group(g, carry):
        for t in range(2):
            local(g, t).wait()
            load(g, t).wait()
        for o in range(1, REACH + 1):
            @pl.when(has_prev[o])
            def _():
                for j in range(heads):
                    for t in range(2):
                        onward(g, t, j, o).wait_recv()

            if o == 1:
                @pl.when(relays)
                def _():
                    for j in range(heads):
                        for t in range(2):
                            relay(g, t, j).start()
        c = cols(g * D, D)
        keys = jnp.concatenate([kv[o, 0, :, c] for o in order], 0)
        values = jnp.concatenate([kv[o, 1, :, c] for o in order], 0)
        heads_q = []
        first_q = g * qw
        for u in range(GROUP // PAIR):
            spans = [cols(first_q + u * lanes + i * D, D) for i in range(PAIR)]
            q = jnp.concatenate([q_vm[:, s] for s in spans], 0)
            do = jnp.concatenate([do_vm[:, s] for s in spans], 0)
            heads_q.append((q, do, nt(keys, q), nt(values, do)))
        unit = scale * math.log2(math.e)
        for u, (q, do, scores, d_w) in enumerate(heads_q):
            s_own = jnp.where(wide_lower, scores[:length], scores[length:2 * length]) + bias[0]
            s_prev = scores[2 * length:] + bias[1]
            top = jnp.maximum(
                jnp.max(s_own, 0, keepdims=True), jnp.max(s_prev, 0, keepdims=True)
            )
            e_own = jnp.exp2((s_own - top) * unit)
            e_prev = jnp.exp2((s_prev - top) * unit)
            inv = 1.0 / (
                jnp.sum(e_own, 0, keepdims=True) + jnp.sum(e_prev, 0, keepdims=True)
            )
            w_own = e_own * inv
            w_prev = e_prev * inv
            d_own = jnp.where(wide_lower, d_w[:length], d_w[length:2 * length])
            d_prev = d_w[2 * length:]
            delta = jnp.sum(w_own * d_own, 0, keepdims=True) + jnp.sum(
                w_prev * d_prev, 0, keepdims=True
            )
            r_own = w_own.astype(jnp.bfloat16)
            g_own = (w_own * (d_own - delta)).astype(jnp.bfloat16)
            keep = low[...]
            r_low = r_own * keep
            g_low = g_own * keep
            lane = slice(u * lanes, (u + 1) * lanes)
            w_vm[g, :length, lane] = r_low
            w_vm[g, length:2 * length, lane] = r_own - r_low
            w_vm[g, 2 * length:, lane] = w_prev.astype(jnp.bfloat16)
            ds_vm[g, :length, lane] = g_low
            ds_vm[g, length:2 * length, lane] = g_own - g_low
            ds_vm[g, 2 * length:, lane] = (w_prev * (d_prev - delta)).astype(jnp.bfloat16)
        dk_sum = nn(ds_vm[g], jnp.concatenate([h[0] for h in heads_q], 0))
        dv_sum = nn(w_vm[g], jnp.concatenate([h[1] for h in heads_q], 0))
        for t, total in enumerate((dk_sum * scale, dv_sum)):
            for at, o in enumerate(order):
                block = total[at * length:(at + 1) * length]
                if o == 0:
                    own[t, :, c] = block
                elif o == 1:
                    hold[t, :, c] = block
                else:
                    stage[1, t, :, c] = block.astype(jnp.bfloat16)

        @pl.when(relays)
        def _():
            for t in range(2):
                back(g, t, 2).start()

            @pl.when(g >= 1)
            def _():
                merge(g - 1)

        @pl.when(jnp.logical_and(odd, has_prev[2]))
        def _():
            for t in range(2):
                back_near(g, t).start()

        @pl.when(odd)
        def _():
            for t in range(2):
                stage[0, t, :, c] = hold[t, :, c].astype(jnp.bfloat16)
                back(g, t, 1).start()
        return carry

    def outputs(g, carry):
        c = cols(g * D, D)
        for t, src, dst, by in ((1, w_vm, att_ref, None), (0, ds_vm, dq_ref, scale)):
            flat = jnp.transpose(jnp.concatenate([kv[o, t, :, c] for o in order], 0))
            for u in range(GROUP // PAIR):
                made = nn(flat, src[g, :, u * lanes:(u + 1) * lanes])
                if by is not None:
                    made = made * by
                made = jnp.transpose(made.astype(jnp.bfloat16))
                for i in range(PAIR):
                    span = cols(g * qw + u * lanes + i * D, D)
                    dst[:, span] = made[i * length:(i + 1) * length]
        return carry

    lax.fori_loop(0, groups, one_group, 0)
    lax.fori_loop(0, groups // 2, outputs, 0)

    @pl.when(relays)
    def _():
        merge(groups - 1)

    lax.fori_loop(groups // 2, groups, outputs, 0)

    for g in range(groups):
        c = cols(g * D, D)
        for o in range(1, REACH + 1):
            @pl.when(deals_next[o])
            def _():
                for t in range(2):
                    back(g, t, o).wait_recv()
        for t in range(2):
            total = own[t, :, c]
            for o in range(1, REACH + 1):
                total = total + got[o - 1, t, :, c].astype(jnp.float32)
            final[t, :, c] = total.astype(jnp.bfloat16)
            for j in range(1, heads):
                home(g, t, j).start()
            stay(g, t).start()

    for g in range(groups):
        for t in range(2):
            stay(g, t).wait()
            for j in range(1, heads):
                across(g, t, j).wait_send()
                home(g, t, j).wait()
        for o in range(1, REACH + 1):
            @pl.when(deals_next[o])
            def _():
                for j in range(heads):
                    for t in range(2):
                        onward(g, t, j, o).wait_send()

            @pl.when(has_prev[o])
            def _():
                for t in range(2):
                    back(g, t, o).wait_send()

        @pl.when(relays)
        def _():
            for j in range(heads):
                for t in range(2):
                    relay(g, t, j).wait_send()


def write_out(*refs):
    count = len(refs) // 2
    sems = refs[-1]
    copies = []
    for i in range(count):
        src, dst = refs[i], refs[count + i]
        half = src.shape[0] // 2
        for k in range(2):
            r = pl.ds(k * half, half)
            copies.append(pltpu.make_async_copy(src.at[r], dst.at[r], sems.at[i, k]))
    for copy in copies:
        copy.start()
    for copy in copies:
        copy.wait()


def body(mesh, query, key, value, output_cotangent, segment):
    length, wide = query.shape
    part, kv_wide = key.shape
    heads = mesh.shape["head"]
    inners = mesh.shape["inner"]
    shards = mesh.shape["outer"] * inners
    groups = kv_wide // heads // HEAD_SIZE
    width = groups * HEAD_SIZE
    bf, f32 = jnp.bfloat16, jnp.float32
    dma = pltpu.SemaphoreType.DMA
    peers = max(heads - 1, 1)
    lanes = PAIR * HEAD_SIZE
    shapes = ((length, wide), (length, wide), (part, kv_wide), (part, kv_wide))
    operands = (query, key, value, output_cotangent, segment.reshape(shards, length))
    results = pl.pallas_call(
        functools.partial(kernel, inners, shards, heads),
        out_shape=tuple(pltpu.VMEM(shape, bf) for shape in shapes),
        in_specs=[pl.BlockSpec(memory_space=pltpu.HBM)] * 5,
        out_specs=[pl.BlockSpec(memory_space=pltpu.VMEM)] * 4,
        scratch_shapes=[
            pltpu.VMEM((length, wide), bf),
            pltpu.VMEM((length, wide), bf),
            pltpu.VMEM((shards, length), jnp.int32),
            pltpu.VMEM((REACH + 1, 2, length, width), bf),
            pltpu.VMEM((2, length, width), f32),
            pltpu.VMEM((2, length, width), f32),
            pltpu.VMEM((2, length, width), bf),
            pltpu.VMEM((REACH, 2, length, width), bf),
            pltpu.VMEM((REACH, 2, length, width), bf),
            pltpu.VMEM((2, length, width), bf),
            pltpu.VMEM((2, length, lanes), f32),
            pltpu.VMEM((length, lanes), bf),
            pltpu.VMEM((groups, (REACH + 1) * length, GROUP * HEAD_SIZE), bf),
            pltpu.VMEM((groups, (REACH + 1) * length, GROUP * HEAD_SIZE), bf),
            dma((2, groups)),
            dma(()),
            dma((2, groups)),
            dma((peers, 2, groups)),
            dma((peers, 2, groups)),
            dma((REACH, heads, 2, groups)),
            dma((REACH, heads, 2, groups)),
            dma((heads, 2, groups)),
            dma((2, groups)),
            dma((REACH, 2, groups)),
            dma((REACH, 2, groups)),
            dma((peers, 2, groups)),
            dma((peers, 2, groups)),
            dma((2, groups)),
        ],
        compiler_params=pltpu.CompilerParams(
            collective_id=0, has_side_effects=True, vmem_limit_bytes=61 * 2**20
        ),
        name="packed_attention",
    )(*(pltpu.with_memory_space_constraint(x, pltpu.HBM) for x in operands))
    return pl.pallas_call(
        write_out,
        out_shape=tuple(jax.ShapeDtypeStruct(shape, bf) for shape in shapes),
        in_specs=[pl.BlockSpec(memory_space=pltpu.VMEM)] * 4,
        out_specs=[pl.BlockSpec(memory_space=pltpu.HBM)] * 4,
        scratch_shapes=[dma((len(shapes), 2))],
        name="write_out",
    )(*results)


def solution(mesh):
    in_specs = (
        P(("outer", "inner"), "head"),
        P(("outer", "inner", "head"), None),
        P(("outer", "inner", "head"), None),
        P(("outer", "inner"), "head"),
        P(),
    )
    out_specs = (
        P(("outer", "inner"), "head"),
        P(("outer", "inner"), "head"),
        P(("outer", "inner", "head"), None),
        P(("outer", "inner", "head"), None),
    )
    return jax.shard_map(
        functools.partial(body, mesh),
        mesh=mesh, in_specs=in_specs, out_specs=out_specs, check_vma=False,
    )
```

```python
import functools
import math

import jax
import jax.numpy as jnp
from jax import lax
from jax.experimental import pallas as pl
from jax.experimental.pallas import tpu as pltpu
from jax.sharding import PartitionSpec as P

QUERY_HEADS = 48
KEY_VALUE_HEADS = 8
HEAD_SIZE = 128
REACH = 2
GROUP = QUERY_HEADS // KEY_VALUE_HEADS
PAIR = 2
MESH = pl.DeviceIdType.MESH


def nt(a, b):
    return lax.dot_general(a, b, (((1,), (1,)), ((), ())), preferred_element_type=jnp.float32)


def tn(a, b):
    return lax.dot_general(a, b, (((0,), (0,)), ((), ())), preferred_element_type=jnp.float32)


def nn(a, b):
    return lax.dot_general(a, b, (((1,), (0,)), ((), ())), preferred_element_type=jnp.float32)


ORDER = (0, 2, 1)


def outputs(kv, w_vm, ds_vm, att, dq, base, g, carry):
    D = HEAD_SIZE
    length = kv.shape[2]
    lanes = PAIR * D
    c = pl.ds(pl.multiple_of(g * D, D), D)
    for t, src, dst, by in ((1, w_vm, att, None), (0, ds_vm, dq, 1.0 / math.sqrt(D))):
        flat = jnp.transpose(jnp.concatenate([kv[o, t, :, c] for o in ORDER], 0))
        for u in range(GROUP // PAIR):
            made = nn(flat, src[g, :, u * lanes:(u + 1) * lanes])
            if by is not None:
                made = made * by
            made = jnp.transpose(made.astype(jnp.bfloat16))
            for i in range(PAIR):
                start = (g - base) * GROUP * D + u * lanes + i * D
                dst[:, pl.ds(pl.multiple_of(start, D), D)] = made[i * length:(i + 1) * length]
    return carry


def kernel(
    inners, shards, heads,
    query_ref, key_ref, value_ref, cot_ref, seg_ref,
    att_ref, dq_ref, dk_ref, dv_ref, w_vm, ds_vm, kv,
    q_vm, do_vm, seg_vm, own, hold, mid, stage, got, final, bias, low,
    in_sem, seg_sem, loc_sem,
    y_send, y_recv, f_send, f_recv, r_send, m_recv, b_send, b_recv, z_send, z_recv, z_loc,
):
    D = HEAD_SIZE
    length = q_vm.shape[0]
    groups = kv.shape[3] // D
    width = groups * D
    part = length // heads
    qw = GROUP * D
    lanes = PAIR * D
    scale = 1.0 / math.sqrt(D)
    shard = lax.axis_index("outer") * inners + lax.axis_index("inner")
    me = lax.axis_index("head")

    def at_shard(target):
        return {"outer": lax.div(target, inners), "inner": lax.rem(target, inners), "head": me}

    def at_head(target):
        return {"head": target}

    def rows(p):
        return pl.ds(pl.multiple_of(p * part, part), part)

    def cols(start, size):
        return pl.ds(pl.multiple_of(start, D), size)

    def before(j):
        return lax.rem(me + heads - j, heads)

    def after(j):
        return lax.rem(me + j, heads)

    both = (key_ref, value_ref)
    outs = (dk_ref, dv_ref)

    def load(g, which):
        src, dst = ((query_ref, q_vm), (cot_ref, do_vm))[which]
        c = cols(g * qw, qw)
        return pltpu.make_async_copy(src.at[:, c], dst.at[:, c], in_sem.at[which, g])

    def local(g, t):
        return pltpu.make_async_copy(
            both[t].at[:, cols(me * width + g * D, D)],
            kv.at[0, t, rows(me), cols(g * D, D)],
            loc_sem.at[t, g],
        )

    def across(g, t, j):
        return pltpu.make_async_remote_copy(
            src_ref=both[t].at[:, cols(after(j) * width + g * D, D)],
            dst_ref=kv.at[0, t, rows(me), cols(g * D, D)],
            send_sem=y_send.at[j - 1, t, g],
            recv_sem=y_recv.at[j - 1, t, g],
            device_id=at_head(after(j)),
            device_id_type=MESH,
        )

    def onward(g, t, j, o):
        r = rows(before(j))
        if j == 0:
            src = both[t].at[:, cols(me * width + g * D, D)]
        else:
            src = kv.at[0, t, r, cols(g * D, D)]
        return pltpu.make_async_remote_copy(
            src_ref=src,
            dst_ref=kv.at[o, t, r, cols(g * D, D)],
            send_sem=f_send.at[o - 1, j, t, g],
            recv_sem=f_recv.at[o - 1, j, t, g],
            device_id=at_shard(shard + o),
            device_id_type=MESH,
        )

    def relay(g, t, j):
        r = rows(before(j))
        return pltpu.make_async_remote_copy(
            src_ref=kv.at[1, t, r, cols(g * D, D)],
            dst_ref=kv.at[2, t, r, cols(g * D, D)],
            send_sem=r_send.at[j, t, g],
            recv_sem=f_recv.at[1, j, t, g],
            device_id=at_shard(shard + 1),
            device_id_type=MESH,
        )

    def back_near(g, t):
        return pltpu.make_async_remote_copy(
            src_ref=stage.at[1, t, :, cols(g * D, D)],
            dst_ref=mid.at[t, :, cols(g * D, D)],
            send_sem=b_send.at[1, t, g],
            recv_sem=m_recv.at[t, g],
            device_id=at_shard(shard - 1),
            device_id_type=MESH,
        )

    def back(g, t, o):
        return pltpu.make_async_remote_copy(
            src_ref=stage.at[o - 1, t, :, cols(g * D, D)],
            dst_ref=got.at[o - 1, t, :, cols(g * D, D)],
            send_sem=b_send.at[o - 1, t, g],
            recv_sem=b_recv.at[o - 1, t, g],
            device_id=at_shard(shard - o),
            device_id_type=MESH,
        )

    def home(g, t, j):
        return pltpu.make_async_remote_copy(
            src_ref=final.at[t, rows(after(j)), cols(g * D, D)],
            dst_ref=outs[t].at[:, cols(me * width + g * D, D)],
            send_sem=z_send.at[j - 1, t, g],
            recv_sem=z_recv.at[j - 1, t, g],
            device_id=at_head(after(j)),
            device_id_type=MESH,
        )

    def stay(g, t):
        return pltpu.make_async_copy(
            final.at[t, rows(me), cols(g * D, D)],
            outs[t].at[:, cols(me * width + g * D, D)],
            z_loc.at[t, g],
        )

    has_next = [None] + [shard + o < shards for o in range(1, REACH + 1)]
    has_prev = [None] + [shard >= o for o in range(1, REACH + 1)]

    even = lax.rem(shard, 2) == 0
    odd = jnp.logical_not(even)
    deals_next = [None, has_next[1], jnp.logical_and(even, has_next[2])]
    deals_prev = [None, has_prev[1], jnp.logical_and(even, has_prev[2])]
    relays = deals_prev[2]

    barrier = pltpu.get_barrier_semaphore()
    for j in range(1, heads):
        pl.semaphore_signal(barrier, inc=1, device_id=at_head(after(j)), device_id_type=MESH)
    for o in range(1, REACH + 1):
        @pl.when(deals_next[o])
        def _():
            pl.semaphore_signal(barrier, inc=1, device_id=at_shard(shard + o), device_id_type=MESH)

        @pl.when(deals_prev[o])
        def _():
            pl.semaphore_signal(barrier, inc=1, device_id=at_shard(shard - o), device_id_type=MESH)

    seg_copy = pltpu.make_async_copy(seg_ref, seg_vm, seg_sem)
    seg_copy.start()
    for g in range(groups):
        for t in range(2):
            local(g, t).start()
            load(g, t).start()

    for o in range(1, REACH + 1):
        @pl.when(jnp.logical_not(has_prev[o]))
        def _():
            kv[o] = jnp.zeros(kv.shape[1:], kv.dtype)

        @pl.when(jnp.logical_not(deals_next[o]))
        def _():
            got[o - 1] = jnp.zeros(got.shape[1:], got.dtype)

    partners = heads - 1
    for o in range(1, REACH + 1):
        partners = partners + jnp.where(deals_next[o], 1, 0) + jnp.where(deals_prev[o], 1, 0)
    pl.semaphore_wait(barrier, partners)

    for g in range(groups):
        for t in range(2):
            for j in range(1, heads):
                across(g, t, j).start()
        for o in range(REACH, 0, -1):
            @pl.when(deals_next[o])
            def _():
                for t in range(2):
                    onward(g, t, 0, o).start()

    seg_copy.wait()

    def seg_row(o):
        row = seg_vm[pl.ds(jnp.maximum(shard - o, 0), 1), :]
        return jnp.where(shard >= o, row, -1)

    def tall(row):
        return jnp.transpose(jnp.broadcast_to(row, (length, length)))

    seg_here = seg_row(0)
    key_index = lax.broadcasted_iota(jnp.int32, (length, length), 0)
    query_index = lax.broadcasted_iota(jnp.int32, (length, length), 1)
    lower = key_index <= query_index
    merged = jnp.where(lower, tall(seg_here), tall(seg_row(2)))
    blocked = -jnp.inf
    bias_own = jnp.where(merged == seg_here, 0.0, blocked)
    bias_prev = jnp.where(tall(seg_row(1)) == seg_here, 0.0, blocked)
    one_low = jnp.where(lower, 1.0, 0.0).astype(jnp.bfloat16)
    for i in range(PAIR):
        bias[0, :, i * D:(i + 1) * D] = bias_own
        bias[1, :, i * D:(i + 1) * D] = bias_prev
        low[:, i * D:(i + 1) * D] = one_low

    for g in range(groups):
        for j in range(1, heads):
            for t in range(2):
                across(g, t, j).wait_recv()
            for o in range(REACH, 0, -1):
                @pl.when(deals_next[o])
                def _():
                    for t in range(2):
                        onward(g, t, j, o).start()

    wide_lower = lax.broadcasted_iota(jnp.int32, (length, lanes), 0) <= lax.rem(
        lax.broadcasted_iota(jnp.int32, (length, lanes), 1), D
    )

    def merge(g):
        c = cols(g * D, D)
        for t in range(2):
            back_near(g, t).wait_recv()
            stage[0, t, :, c] = (hold[t, :, c] + mid[t, :, c].astype(jnp.float32)).astype(
                jnp.bfloat16
            )
            back(g, t, 1).start()

    def one_group(g, carry):
        for t in range(2):
            local(g, t).wait()
            load(g, t).wait()
        for o in range(1, REACH + 1):
            @pl.when(has_prev[o])
            def _():
                for j in range(heads):
                    for t in range(2):
                        onward(g, t, j, o).wait_recv()

            if o == 1:
                @pl.when(relays)
                def _():
                    for j in range(heads):
                        for t in range(2):
                            relay(g, t, j).start()
        c = cols(g * D, D)
        keys = jnp.concatenate([kv[o, 0, :, c] for o in ORDER], 0)
        values = jnp.concatenate([kv[o, 1, :, c] for o in ORDER], 0)
        heads_q = []
        first_q = g * qw
        for u in range(GROUP // PAIR):
            spans = [cols(first_q + u * lanes + i * D, D) for i in range(PAIR)]
            q = jnp.concatenate([q_vm[:, s] for s in spans], 0)
            do = jnp.concatenate([do_vm[:, s] for s in spans], 0)
            heads_q.append((q, do, nt(keys, q), nt(values, do)))
        unit = scale * math.log2(math.e)
        for u, (q, do, scores, d_w) in enumerate(heads_q):
            s_own = jnp.where(wide_lower, scores[:length], scores[length:2 * length]) + bias[0]
            s_prev = scores[2 * length:] + bias[1]
            top = jnp.maximum(
                jnp.max(s_own, 0, keepdims=True), jnp.max(s_prev, 0, keepdims=True)
            )
            e_own = jnp.exp2((s_own - top) * unit)
            e_prev = jnp.exp2((s_prev - top) * unit)
            inv = 1.0 / (
                jnp.sum(e_own, 0, keepdims=True) + jnp.sum(e_prev, 0, keepdims=True)
            )
            w_own = e_own * inv
            w_prev = e_prev * inv
            d_own = jnp.where(wide_lower, d_w[:length], d_w[length:2 * length])
            d_prev = d_w[2 * length:]
            delta = jnp.sum(w_own * d_own, 0, keepdims=True) + jnp.sum(
                w_prev * d_prev, 0, keepdims=True
            )
            r_own = w_own.astype(jnp.bfloat16)
            g_own = (w_own * (d_own - delta)).astype(jnp.bfloat16)
            keep = low[...]
            r_low = r_own * keep
            g_low = g_own * keep
            lane = slice(u * lanes, (u + 1) * lanes)
            w_vm[g, :length, lane] = r_low
            w_vm[g, length:2 * length, lane] = r_own - r_low
            w_vm[g, 2 * length:, lane] = w_prev.astype(jnp.bfloat16)
            ds_vm[g, :length, lane] = g_low
            ds_vm[g, length:2 * length, lane] = g_own - g_low
            ds_vm[g, 2 * length:, lane] = (w_prev * (d_prev - delta)).astype(jnp.bfloat16)
        dk_sum = nn(ds_vm[g], jnp.concatenate([h[0] for h in heads_q], 0))
        dv_sum = nn(w_vm[g], jnp.concatenate([h[1] for h in heads_q], 0))
        for t, total in enumerate((dk_sum * scale, dv_sum)):
            for at, o in enumerate(ORDER):
                block = total[at * length:(at + 1) * length]
                if o == 0:
                    own[t, :, c] = block
                elif o == 1:
                    hold[t, :, c] = block
                else:
                    stage[1, t, :, c] = block.astype(jnp.bfloat16)

        @pl.when(relays)
        def _():
            for t in range(2):
                back(g, t, 2).start()

            @pl.when(g >= 1)
            def _():
                merge(g - 1)

        @pl.when(jnp.logical_and(odd, has_prev[2]))
        def _():
            for t in range(2):
                back_near(g, t).start()

        @pl.when(odd)
        def _():
            for t in range(2):
                stage[0, t, :, c] = hold[t, :, c].astype(jnp.bfloat16)
                back(g, t, 1).start()
        return carry

    lax.fori_loop(0, groups, one_group, 0)
    lax.fori_loop(0, groups // 2, functools.partial(outputs, kv, w_vm, ds_vm, att_ref, dq_ref, 0), 0)

    @pl.when(relays)
    def _():
        merge(groups - 1)

    for g in range(groups):
        c = cols(g * D, D)
        for o in range(1, REACH + 1):
            @pl.when(deals_next[o])
            def _():
                for t in range(2):
                    back(g, t, o).wait_recv()
        for t in range(2):
            total = own[t, :, c]
            for o in range(1, REACH + 1):
                total = total + got[o - 1, t, :, c].astype(jnp.float32)
            final[t, :, c] = total.astype(jnp.bfloat16)
            for j in range(1, heads):
                home(g, t, j).start()
            stay(g, t).start()

    for g in range(groups):
        for t in range(2):
            stay(g, t).wait()
            for j in range(1, heads):
                across(g, t, j).wait_send()
                home(g, t, j).wait()
        for o in range(1, REACH + 1):
            @pl.when(deals_next[o])
            def _():
                for j in range(heads):
                    for t in range(2):
                        onward(g, t, j, o).wait_send()

            @pl.when(has_prev[o])
            def _():
                for t in range(2):
                    back(g, t, o).wait_send()

        @pl.when(relays)
        def _():
            for j in range(heads):
                for t in range(2):
                    relay(g, t, j).wait_send()


def finish(
    att_a, dq_a, dk, dv, w_vm, ds_vm, kv, att_out, dq_out, dk_out, dv_out, att_b, dq_b, sems, late
):
    groups = w_vm.shape[0]
    half = groups // 2
    qw = GROUP * HEAD_SIZE
    early = pl.ds(0, half * qw)
    copies = []
    for i, (src, dst) in enumerate((
        (att_a, att_out.at[:, early]), (dq_a, dq_out.at[:, early]), (dk, dk_out), (dv, dv_out)
    )):
        copies.append(pltpu.make_async_copy(src, dst, sems.at[i]))
        copies[-1].start()

    for g in range(half, groups):
        outputs(kv, w_vm, ds_vm, att_b, dq_b, half, g, 0)
        here, there = pl.ds((g - half) * qw, qw), pl.ds(g * qw, qw)
        for t, (src, dst) in enumerate(((att_b, att_out), (dq_b, dq_out))):
            copies.append(
                pltpu.make_async_copy(src.at[:, here], dst.at[:, there], late.at[t, g - half])
            )
            copies[-1].start()
    for copy in copies:
        copy.wait()


def body(mesh, query, key, value, output_cotangent, segment):
    length, wide = query.shape
    part, kv_wide = key.shape
    heads = mesh.shape["head"]
    inners = mesh.shape["inner"]
    shards = mesh.shape["outer"] * inners
    groups = kv_wide // heads // HEAD_SIZE
    width = groups * HEAD_SIZE
    bf, f32 = jnp.bfloat16, jnp.float32
    dma = pltpu.SemaphoreType.DMA
    peers = max(heads - 1, 1)
    lanes = PAIR * HEAD_SIZE
    shapes = ((length, wide), (length, wide), (part, kv_wide), (part, kv_wide))
    half = groups // 2
    qw = GROUP * HEAD_SIZE
    made = (groups, (REACH + 1) * length, qw)
    passed = (
        (length, half * qw), (length, half * qw), (part, kv_wide), (part, kv_wide),
        made, made, (REACH + 1, 2, length, width),
    )
    operands = (query, key, value, output_cotangent, segment.reshape(shards, length))
    results = pl.pallas_call(
        functools.partial(kernel, inners, shards, heads),
        out_shape=tuple(pltpu.VMEM(shape, bf) for shape in passed),
        in_specs=[pl.BlockSpec(memory_space=pltpu.HBM)] * 5,
        out_specs=[pl.BlockSpec(memory_space=pltpu.VMEM)] * len(passed),
        scratch_shapes=[
            pltpu.VMEM((length, wide), bf),
            pltpu.VMEM((length, wide), bf),
            pltpu.VMEM((shards, length), jnp.int32),
            pltpu.VMEM((2, length, width), f32),
            pltpu.VMEM((2, length, width), f32),
            pltpu.VMEM((2, length, width), bf),
            pltpu.VMEM((REACH, 2, length, width), bf),
            pltpu.VMEM((REACH, 2, length, width), bf),
            pltpu.VMEM((2, length, width), bf),
            pltpu.VMEM((2, length, lanes), f32),
            pltpu.VMEM((length, lanes), bf),
            dma((2, groups)),
            dma(()),
            dma((2, groups)),
            dma((peers, 2, groups)),
            dma((peers, 2, groups)),
            dma((REACH, heads, 2, groups)),
            dma((REACH, heads, 2, groups)),
            dma((heads, 2, groups)),
            dma((2, groups)),
            dma((REACH, 2, groups)),
            dma((REACH, 2, groups)),
            dma((peers, 2, groups)),
            dma((peers, 2, groups)),
            dma((2, groups)),
        ],
        compiler_params=pltpu.CompilerParams(
            collective_id=0, has_side_effects=True, vmem_limit_bytes=40 * 2**20
        ),
        name="packed_attention",
    )(*(pltpu.with_memory_space_constraint(x, pltpu.HBM) for x in operands))
    return pl.pallas_call(
        finish,
        out_shape=tuple(jax.ShapeDtypeStruct(shape, bf) for shape in shapes),
        in_specs=[pl.BlockSpec(memory_space=pltpu.VMEM)] * len(passed),
        out_specs=[pl.BlockSpec(memory_space=pltpu.HBM)] * 4,
        scratch_shapes=[
            pltpu.VMEM((length, wide - half * qw), bf),
            pltpu.VMEM((length, wide - half * qw), bf),
            dma((4,)),
            dma((2, groups - half)),
        ],
        compiler_params=pltpu.CompilerParams(vmem_limit_bytes=16 * 2**20),
        name="finish",
    )(*results)


def solution(mesh):
    in_specs = (
        P(("outer", "inner"), "head"),
        P(("outer", "inner", "head"), None),
        P(("outer", "inner", "head"), None),
        P(("outer", "inner"), "head"),
        P(),
    )
    out_specs = (
        P(("outer", "inner"), "head"),
        P(("outer", "inner"), "head"),
        P(("outer", "inner", "head"), None),
        P(("outer", "inner", "head"), None),
    )
    return jax.shard_map(
        functools.partial(body, mesh),
        mesh=mesh, in_specs=in_specs, out_specs=out_specs, check_vma=False,
    )
```

```python
import functools
import math

import jax
import jax.numpy as jnp
from jax import lax
from jax.experimental import pallas as pl
from jax.experimental.pallas import tpu as pltpu
from jax.sharding import PartitionSpec as P

QUERY_HEADS = 48
KEY_VALUE_HEADS = 8
HEAD_SIZE = 128
REACH = 2
GROUP = QUERY_HEADS // KEY_VALUE_HEADS
PAIR = 2
MESH = pl.DeviceIdType.MESH


def nt(a, b):
    return lax.dot_general(a, b, (((1,), (1,)), ((), ())), preferred_element_type=jnp.float32)


def tn(a, b):
    return lax.dot_general(a, b, (((0,), (0,)), ((), ())), preferred_element_type=jnp.float32)


def nn(a, b):
    return lax.dot_general(a, b, (((1,), (0,)), ((), ())), preferred_element_type=jnp.float32)


ORDER = (0, 2, 1)


def outputs(kv, w_vm, ds_vm, att, dq, base, g, carry):
    D = HEAD_SIZE
    length = kv.shape[3]
    lanes = PAIR * D
    for t, src, dst, by in ((1, w_vm, att, None), (0, ds_vm, dq, 1.0 / math.sqrt(D))):
        flat = jnp.transpose(jnp.concatenate([kv[o, g, t] for o in ORDER], 0))
        for u in range(GROUP // PAIR):
            made = nn(flat, src[g, :, u * lanes:(u + 1) * lanes])
            if by is not None:
                made = made * by
            made = jnp.transpose(made.astype(jnp.bfloat16))
            for i in range(PAIR):
                start = (g - base) * GROUP * D + u * lanes + i * D
                dst[:, pl.ds(pl.multiple_of(start, D), D)] = made[i * length:(i + 1) * length]
    return carry


def kernel(
    inners, shards, heads,
    query_ref, key_ref, value_ref, cot_ref, seg_ref,
    att_ref, dq_ref, dkv_ref, w_vm, ds_vm, kv,
    q_vm, do_vm, seg_vm, flat_vm, own_kv, own, hold, mid, stage, got, final, bias, low,
    in_sem, seg_sem, kv_sem,
    y_send, y_recv, f_send, f_recv, r_send, m_recv, b_send, b_recv, z_send, z_recv,
):
    D = HEAD_SIZE
    length = q_vm.shape[0]
    groups = kv.shape[1]
    part = length // heads
    qw = GROUP * D
    lanes = PAIR * D
    scale = 1.0 / math.sqrt(D)
    shard = lax.axis_index("outer") * inners + lax.axis_index("inner")
    me = lax.axis_index("head")

    def at_shard(target):
        return {"outer": lax.div(target, inners), "inner": lax.rem(target, inners), "head": me}

    def at_head(target):
        return {"head": target}

    def rows(p):
        return pl.ds(pl.multiple_of(p * part, part), part)

    def cols(start, size):
        return pl.ds(pl.multiple_of(start, D), size)

    def before(j):
        return lax.rem(me + heads - j, heads)

    def after(j):
        return lax.rem(me + j, heads)

    def remote(src, dst, send, recv, target):
        return pltpu.make_async_remote_copy(
            src_ref=src, dst_ref=dst, send_sem=send, recv_sem=recv,
            device_id=target, device_id_type=MESH,
        )

    def load(g, which):
        src, dst = ((query_ref, q_vm), (cot_ref, do_vm))[which]
        c = cols(g * qw, qw)
        return pltpu.make_async_copy(src.at[:, c], dst.at[:, c], in_sem.at[which, g])

    def across(g, j):
        return remote(
            own_kv.at[after(j) * groups + g], kv.at[0, g, :, rows(me)],
            y_send.at[j - 1], y_recv.at[j - 1, g], at_head(after(j)),
        )

    def onward(g, j, o):
        r = rows(before(j))
        src = own_kv.at[me * groups + g] if j == 0 else kv.at[0, g, :, r]
        return remote(
            src, kv.at[o, g, :, r], f_send.at[o - 1], f_recv.at[o - 1, g], at_shard(shard + o)
        )

    def onward_all(g, o):
        return remote(
            kv.at[0, g], kv.at[o, g], f_send.at[o - 1], f_recv.at[o - 1, g], at_shard(shard + o)
        )

    def relay(g):
        return remote(
            kv.at[1, g], kv.at[2, g], r_send, f_recv.at[1, g], at_shard(shard + 1)
        )

    def back_near(g):
        return remote(stage.at[1, g], mid.at[g], b_send.at[1], m_recv.at[g], at_shard(shard - 1))

    def back(g, o):
        return remote(
            stage.at[o - 1, g], got.at[o - 1, g], b_send.at[o - 1], b_recv.at[o - 1, g],
            at_shard(shard - o),
        )

    def home(g, j):
        return remote(
            final.at[g, :, rows(after(j))], dkv_ref.at[me * groups + g],
            z_send.at[j - 1], z_recv.at[j - 1], at_head(after(j)),
        )

    has_next = [None] + [shard + o < shards for o in range(1, REACH + 1)]
    has_prev = [None] + [shard >= o for o in range(1, REACH + 1)]

    even = lax.rem(shard, 2) == 0
    odd = jnp.logical_not(even)
    deals_next = [None, has_next[1], jnp.logical_and(even, has_next[2])]
    deals_prev = [None, has_prev[1], jnp.logical_and(even, has_prev[2])]
    relays = deals_prev[2]

    barrier = pltpu.get_barrier_semaphore()
    for j in range(1, heads):
        pl.semaphore_signal(barrier, inc=1, device_id=at_head(after(j)), device_id_type=MESH)
    for o in range(1, REACH + 1):
        @pl.when(deals_next[o])
        def _():
            pl.semaphore_signal(barrier, inc=1, device_id=at_shard(shard + o), device_id_type=MESH)

        @pl.when(deals_prev[o])
        def _():
            pl.semaphore_signal(barrier, inc=1, device_id=at_shard(shard - o), device_id_type=MESH)

    kv_loads = [
        pltpu.make_async_copy(ref, flat_vm.at[t], kv_sem.at[t])
        for t, ref in enumerate((key_ref, value_ref))
    ]
    for copy in kv_loads:
        copy.start()
    seg_copy = pltpu.make_async_copy(seg_ref, seg_vm, seg_sem)
    seg_copy.start()
    for g in range(groups):
        for t in range(2):
            load(g, t).start()

    for t in range(2):
        kv_loads[t].wait()
        for h in range(groups * heads):
            own_kv[h, t] = flat_vm[t, :, h * D:(h + 1) * D]

    partners = heads - 1
    for o in range(1, REACH + 1):
        partners = partners + jnp.where(deals_next[o], 1, 0) + jnp.where(deals_prev[o], 1, 0)
    pl.semaphore_wait(barrier, partners)

    for g in range(groups):
        for j in range(1, heads):
            across(g, j).start()
        for o in range(REACH, 0, -1):
            @pl.when(deals_next[o])
            def _():
                onward(g, 0, o).start()

    for g in range(groups):
        for t in range(2):
            kv[0, g, t, rows(me)] = own_kv[me * groups + g, t]
    for o in range(1, REACH + 1):
        @pl.when(jnp.logical_not(has_prev[o]))
        def _():
            kv[o] = jnp.zeros(kv.shape[1:], kv.dtype)

        @pl.when(jnp.logical_not(deals_next[o]))
        def _():
            got[o - 1] = jnp.zeros(got.shape[1:], got.dtype)

    seg_copy.wait()

    def seg_row(o):
        row = seg_vm[pl.ds(jnp.maximum(shard - o, 0), 1), :]
        return jnp.where(shard >= o, row, -1)

    def tall(row):
        return jnp.transpose(jnp.broadcast_to(row, (length, length)))

    seg_here = seg_row(0)
    key_index = lax.broadcasted_iota(jnp.int32, (length, length), 0)
    query_index = lax.broadcasted_iota(jnp.int32, (length, length), 1)
    lower = key_index <= query_index
    merged = jnp.where(lower, tall(seg_here), tall(seg_row(2)))
    blocked = -jnp.inf
    bias_own = jnp.where(merged == seg_here, 0.0, blocked)
    bias_prev = jnp.where(tall(seg_row(1)) == seg_here, 0.0, blocked)
    one_low = jnp.where(lower, 1.0, 0.0).astype(jnp.bfloat16)
    for i in range(PAIR):
        bias[0, :, i * D:(i + 1) * D] = bias_own
        bias[1, :, i * D:(i + 1) * D] = bias_prev
        low[:, i * D:(i + 1) * D] = one_low

    for g in range(groups):
        for j in range(1, heads):
            across(g, j).wait_recv()
            for o in range(REACH, 0, -1):
                @pl.when(deals_next[o])
                def _():
                    onward(g, j, o).start()

    wide_lower = lax.broadcasted_iota(jnp.int32, (length, lanes), 0) <= lax.rem(
        lax.broadcasted_iota(jnp.int32, (length, lanes), 1), D
    )

    def merge(g):
        back_near(g).wait_recv()
        stage[0, g] = (hold[g] + mid[g].astype(jnp.float32)).astype(jnp.bfloat16)
        back(g, 1).start()

    def one_group(g, carry):
        for t in range(2):
            load(g, t).wait()
        for o in range(1, REACH + 1):
            @pl.when(has_prev[o])
            def _():
                onward_all(g, o).wait_recv()

            if o == 1:
                @pl.when(relays)
                def _():
                    relay(g).start()
        keys = jnp.concatenate([kv[o, g, 0] for o in ORDER], 0)
        values = jnp.concatenate([kv[o, g, 1] for o in ORDER], 0)
        heads_q = []
        first_q = g * qw
        for u in range(GROUP // PAIR):
            spans = [cols(first_q + u * lanes + i * D, D) for i in range(PAIR)]
            q = jnp.concatenate([q_vm[:, s] for s in spans], 0)
            do = jnp.concatenate([do_vm[:, s] for s in spans], 0)
            heads_q.append((q, do, nt(keys, q), nt(values, do)))
        unit = scale * math.log2(math.e)
        for u, (q, do, scores, d_w) in enumerate(heads_q):
            s_own = jnp.where(wide_lower, scores[:length], scores[length:2 * length]) + bias[0]
            s_prev = scores[2 * length:] + bias[1]
            top = jnp.maximum(
                jnp.max(s_own, 0, keepdims=True), jnp.max(s_prev, 0, keepdims=True)
            )
            e_own = jnp.exp2((s_own - top) * unit)
            e_prev = jnp.exp2((s_prev - top) * unit)
            inv = 1.0 / (
                jnp.sum(e_own, 0, keepdims=True) + jnp.sum(e_prev, 0, keepdims=True)
            )
            w_own = e_own * inv
            w_prev = e_prev * inv
            d_own = jnp.where(wide_lower, d_w[:length], d_w[length:2 * length])
            d_prev = d_w[2 * length:]
            delta = jnp.sum(w_own * d_own, 0, keepdims=True) + jnp.sum(
                w_prev * d_prev, 0, keepdims=True
            )
            r_own = w_own.astype(jnp.bfloat16)
            g_own = (w_own * (d_own - delta)).astype(jnp.bfloat16)
            keep = low[...]
            r_low = r_own * keep
            g_low = g_own * keep
            lane = slice(u * lanes, (u + 1) * lanes)
            w_vm[g, :length, lane] = r_low
            w_vm[g, length:2 * length, lane] = r_own - r_low
            w_vm[g, 2 * length:, lane] = w_prev.astype(jnp.bfloat16)
            ds_vm[g, :length, lane] = g_low
            ds_vm[g, length:2 * length, lane] = g_own - g_low
            ds_vm[g, 2 * length:, lane] = (w_prev * (d_prev - delta)).astype(jnp.bfloat16)
        dk_sum = nn(ds_vm[g], jnp.concatenate([h[0] for h in heads_q], 0))
        dv_sum = nn(w_vm[g], jnp.concatenate([h[1] for h in heads_q], 0))
        for t, total in enumerate((dk_sum * scale, dv_sum)):
            for at, o in enumerate(ORDER):
                block = total[at * length:(at + 1) * length]
                if o == 0:
                    own[g, t] = block
                elif o == 1:
                    hold[g, t] = block
                else:
                    stage[1, g, t] = block.astype(jnp.bfloat16)

        @pl.when(relays)
        def _():
            back(g, 2).start()

            @pl.when(g >= 1)
            def _():
                merge(g - 1)

        @pl.when(jnp.logical_and(odd, has_prev[2]))
        def _():
            back_near(g).start()

        @pl.when(odd)
        def _():
            stage[0, g] = hold[g].astype(jnp.bfloat16)
            back(g, 1).start()

        return carry

    lax.fori_loop(0, groups, one_group, 0)
    lax.fori_loop(
        0, groups // 2, functools.partial(outputs, kv, w_vm, ds_vm, att_ref, dq_ref, 0), 0
    )

    @pl.when(relays)
    def _():
        merge(groups - 1)

    for g in range(groups):
        for o in range(1, REACH + 1):
            @pl.when(deals_next[o])
            def _():
                back(g, o).wait_recv()
        total = own[g]
        for o in range(1, REACH + 1):
            total = total + got[o - 1, g].astype(jnp.float32)
        final[g] = total.astype(jnp.bfloat16)
        for j in range(1, heads):
            home(g, j).start()
        dkv_ref[me * groups + g] = final[g, :, rows(me)]

    for j in range(1, heads):
        share = own_kv.at[pl.ds(0, groups)]
        remote(share, share, y_send.at[j - 1], y_recv.at[j - 1, 0], at_head(after(j))).wait_send()
        landed = dkv_ref.at[pl.ds(0, groups)]
        ends = remote(share, landed, z_send.at[j - 1], z_recv.at[j - 1], at_head(after(j)))
        ends.wait_send()
        ends.wait_recv()
    for o in range(1, REACH + 1):
        @pl.when(deals_next[o])
        def _():
            remote(
                kv.at[0], kv.at[o], f_send.at[o - 1], f_recv.at[o - 1, 0], at_shard(shard + o)
            ).wait_send()

        @pl.when(has_prev[o])
        def _():
            remote(
                stage.at[o - 1], got.at[o - 1], b_send.at[o - 1], b_recv.at[o - 1, 0],
                at_shard(shard - o),
            ).wait_send()

    @pl.when(relays)
    def _():
        remote(kv.at[1], kv.at[2], r_send, f_recv.at[1, 0], at_shard(shard + 1)).wait_send()


def finish(
    att_a, dq_a, dkv, w_vm, ds_vm, kv, att_out, dq_out, dk_out, dv_out,
    att_b, dq_b, flat, sems, late
):
    groups = w_vm.shape[0]
    half = groups // 2
    qw = GROUP * HEAD_SIZE
    early = pl.ds(0, half * qw)
    copies = []
    for i, (src, dst) in enumerate((
        (att_a, att_out.at[:, early]), (dq_a, dq_out.at[:, early]),
        (flat.at[0], dk_out), (flat.at[1], dv_out),
    )):
        if i >= 2:
            for h in range(dkv.shape[0]):
                flat[i - 2, :, h * HEAD_SIZE:(h + 1) * HEAD_SIZE] = dkv[h, i - 2]
        copies.append(pltpu.make_async_copy(src, dst, sems.at[i]))
        copies[-1].start()

    for g in range(half, groups):
        outputs(kv, w_vm, ds_vm, att_b, dq_b, half, g, 0)
        here, there = pl.ds((g - half) * qw, qw), pl.ds(g * qw, qw)
        for t, (src, dst) in enumerate(((att_b, att_out), (dq_b, dq_out))):
            copies.append(
                pltpu.make_async_copy(src.at[:, here], dst.at[:, there], late.at[t, g - half])
            )
            copies[-1].start()
    for copy in copies:
        copy.wait()


def body(mesh, query, key, value, output_cotangent, segment):
    length, wide = query.shape
    part, kv_wide = key.shape
    heads = mesh.shape["head"]
    inners = mesh.shape["inner"]
    shards = mesh.shape["outer"] * inners
    groups = kv_wide // heads // HEAD_SIZE
    bf, f32 = jnp.bfloat16, jnp.float32
    dma = pltpu.SemaphoreType.DMA
    peers = max(heads - 1, 1)
    lanes = PAIR * HEAD_SIZE
    shapes = ((length, wide), (length, wide), (part, kv_wide), (part, kv_wide))
    half = groups // 2
    qw = GROUP * HEAD_SIZE
    block = (groups, 2, length, HEAD_SIZE)
    made = (groups, (REACH + 1) * length, qw)
    passed = (
        (length, half * qw), (length, half * qw), (groups * heads, 2, part, HEAD_SIZE),
        made, made, (REACH + 1, groups, 2, length, HEAD_SIZE),
    )
    operands = (query, key, value, output_cotangent, segment.reshape(shards, length))
    results = pl.pallas_call(
        functools.partial(kernel, inners, shards, heads),
        out_shape=tuple(pltpu.VMEM(shape, bf) for shape in passed),
        in_specs=[pl.BlockSpec(memory_space=pltpu.HBM)] * 5,
        out_specs=[pl.BlockSpec(memory_space=pltpu.VMEM)] * len(passed),
        scratch_shapes=[
            pltpu.VMEM((length, wide), bf),
            pltpu.VMEM((length, wide), bf),
            pltpu.VMEM((shards, length), jnp.int32),
            pltpu.VMEM((2, part, kv_wide), bf),
            pltpu.VMEM((groups * heads, 2, part, HEAD_SIZE), bf),
            pltpu.VMEM(block, f32),
            pltpu.VMEM(block, f32),
            pltpu.VMEM(block, bf),
            pltpu.VMEM((REACH,) + block, bf),
            pltpu.VMEM((REACH,) + block, bf),
            pltpu.VMEM(block, bf),
            pltpu.VMEM((2, length, lanes), f32),
            pltpu.VMEM((length, lanes), bf),
            dma((2, groups)),
            dma(()),
            dma((2,)),
            dma((peers,)),
            dma((peers, groups)),
            dma((REACH,)),
            dma((REACH, groups)),
            dma(()),
            dma((groups,)),
            dma((REACH,)),
            dma((REACH, groups)),
            dma((peers,)),
            dma((peers,)),
        ],
        compiler_params=pltpu.CompilerParams(
            collective_id=0, has_side_effects=True, vmem_limit_bytes=40 * 2**20
        ),
        name="packed_attention",
    )(*(pltpu.with_memory_space_constraint(x, pltpu.HBM) for x in operands))
    return pl.pallas_call(
        finish,
        out_shape=tuple(jax.ShapeDtypeStruct(shape, bf) for shape in shapes),
        in_specs=[pl.BlockSpec(memory_space=pltpu.VMEM)] * len(passed),
        out_specs=[pl.BlockSpec(memory_space=pltpu.HBM)] * 4,
        scratch_shapes=[
            pltpu.VMEM((length, wide - half * qw), bf),
            pltpu.VMEM((length, wide - half * qw), bf),
            pltpu.VMEM((2, part, kv_wide), bf),
            dma((4,)),
            dma((2, groups - half)),
        ],
        compiler_params=pltpu.CompilerParams(vmem_limit_bytes=16 * 2**20),
        name="finish",
    )(*results)


def solution(mesh):
    in_specs = (
        P(("outer", "inner"), "head"),
        P(("outer", "inner", "head"), None),
        P(("outer", "inner", "head"), None),
        P(("outer", "inner"), "head"),
        P(),
    )
    out_specs = (
        P(("outer", "inner"), "head"),
        P(("outer", "inner"), "head"),
        P(("outer", "inner", "head"), None),
        P(("outer", "inner", "head"), None),
    )
    return jax.shard_map(
        functools.partial(body, mesh),
        mesh=mesh, in_specs=in_specs, out_specs=out_specs, check_vma=False,
    )
```

```python
import functools
import math

import jax
import jax.numpy as jnp
from jax import lax
from jax.experimental import pallas as pl
from jax.experimental.pallas import tpu as pltpu
from jax.sharding import PartitionSpec as P

QUERY_HEADS = 48
KEY_VALUE_HEADS = 8
HEAD_SIZE = 128
REACH = 2
GROUP = QUERY_HEADS // KEY_VALUE_HEADS
PAIR = 2
MESH = pl.DeviceIdType.MESH


def nt(a, b):
    return lax.dot_general(a, b, (((1,), (1,)), ((), ())), preferred_element_type=jnp.float32)


def tn(a, b):
    return lax.dot_general(a, b, (((0,), (0,)), ((), ())), preferred_element_type=jnp.float32)


def nn(a, b):
    return lax.dot_general(a, b, (((1,), (0,)), ((), ())), preferred_element_type=jnp.float32)


ORDER = (0, 2, 1)


def outputs(kv, w_vm, ds_vm, att, dq, base, g, carry):
    D = HEAD_SIZE
    length = kv.shape[3]
    lanes = PAIR * D
    for t, src, dst, by in ((1, w_vm, att, None), (0, ds_vm, dq, 1.0 / math.sqrt(D))):
        flat = jnp.transpose(jnp.concatenate([kv[o, g, t] for o in ORDER], 0))
        for u in range(GROUP // PAIR):
            made = nn(flat, src[g, :, u * lanes:(u + 1) * lanes])
            if by is not None:
                made = made * by
            made = jnp.transpose(made.astype(jnp.bfloat16))
            for i in range(PAIR):
                start = (g - base) * GROUP * D + u * lanes + i * D
                dst[:, pl.ds(pl.multiple_of(start, D), D)] = made[i * length:(i + 1) * length]
    return carry


def kernel(
    inners, shards, heads,
    query_ref, key_ref, value_ref, cot_ref, seg_ref,
    att_ref, dq_ref, dkv_ref, w_vm, ds_vm, kv,
    q_vm, do_vm, seg_vm, flat_vm, own_kv, own, hold, mid, stage, got, final, bias, low,
    in_sem, seg_sem, kv_sem,
    y_send, y_recv, f_send, f_recv, r_send, m_recv, b_send, b_recv, z_send, z_recv,
):
    D = HEAD_SIZE
    length = q_vm.shape[0]
    groups = kv.shape[1]
    part = length // heads
    qw = GROUP * D
    lanes = PAIR * D
    scale = 1.0 / math.sqrt(D)
    shard = lax.axis_index("outer") * inners + lax.axis_index("inner")
    me = lax.axis_index("head")

    def at_shard(target):
        return {"outer": lax.div(target, inners), "inner": lax.rem(target, inners), "head": me}

    def at_head(target):
        return {"head": target}

    def rows(p):
        return pl.ds(pl.multiple_of(p * part, part), part)

    def cols(start, size):
        return pl.ds(pl.multiple_of(start, D), size)

    def before(j):
        return lax.rem(me + heads - j, heads)

    def after(j):
        return lax.rem(me + j, heads)

    def remote(src, dst, send, recv, target):
        return pltpu.make_async_remote_copy(
            src_ref=src, dst_ref=dst, send_sem=send, recv_sem=recv,
            device_id=target, device_id_type=MESH,
        )

    def load(g, which):
        src, dst = ((query_ref, q_vm), (cot_ref, do_vm))[which]
        c = cols(g * qw, qw)
        return pltpu.make_async_copy(src.at[:, c], dst.at[:, c], in_sem.at[which, g])

    def across(g, j):
        return remote(
            own_kv.at[after(j) * groups + g], kv.at[0, g, :, rows(me)],
            y_send.at[j - 1], y_recv.at[j - 1, g], at_head(after(j)),
        )

    def onward(g, j, o):
        r = rows(before(j))
        src = own_kv.at[me * groups + g] if j == 0 else kv.at[0, g, :, r]
        return remote(
            src, kv.at[o, g, :, r], f_send.at[o - 1], f_recv.at[o - 1, g], at_shard(shard + o)
        )

    def onward_all(g, o):
        return remote(
            kv.at[0, g], kv.at[o, g], f_send.at[o - 1], f_recv.at[o - 1, g], at_shard(shard + o)
        )

    def relay(g):
        return remote(
            kv.at[1, g], kv.at[2, g], r_send, f_recv.at[1, g], at_shard(shard + 1)
        )

    def back_near(g):
        return remote(stage.at[1, g], mid.at[g], b_send.at[1], m_recv.at[g], at_shard(shard - 1))

    def back(g, o):
        return remote(
            stage.at[o - 1, g], got.at[o - 1, g], b_send.at[o - 1], b_recv.at[o - 1, g],
            at_shard(shard - o),
        )

    def home(g, j):
        return remote(
            final.at[g, :, rows(after(j))], dkv_ref.at[me * groups + g],
            z_send.at[j - 1], z_recv.at[j - 1], at_head(after(j)),
        )

    has_next = [None] + [shard + o < shards for o in range(1, REACH + 1)]
    has_prev = [None] + [shard >= o for o in range(1, REACH + 1)]

    even = lax.rem(shard, 2) == 0
    odd = jnp.logical_not(even)
    even_next = jnp.logical_and(even, has_next[2])
    odd_next = jnp.logical_and(odd, has_next[2])
    relays = jnp.logical_and(even, has_prev[2])
    last = groups - 1

    def sends(g, o):
        return even_next if o == 2 and g > 0 else has_next[o]

    barrier = pltpu.get_barrier_semaphore()
    for j in range(1, heads):
        pl.semaphore_signal(barrier, inc=1, device_id=at_head(after(j)), device_id_type=MESH)
    for o in range(1, REACH + 1):
        @pl.when(has_next[o])
        def _():
            pl.semaphore_signal(barrier, inc=1, device_id=at_shard(shard + o), device_id_type=MESH)

        @pl.when(has_prev[o])
        def _():
            pl.semaphore_signal(barrier, inc=1, device_id=at_shard(shard - o), device_id_type=MESH)

    kv_loads = [
        pltpu.make_async_copy(ref, flat_vm.at[t], kv_sem.at[t])
        for t, ref in enumerate((key_ref, value_ref))
    ]
    for copy in kv_loads:
        copy.start()
    seg_copy = pltpu.make_async_copy(seg_ref, seg_vm, seg_sem)
    seg_copy.start()
    for g in range(groups):
        for t in range(2):
            load(g, t).start()

    for t in range(2):
        kv_loads[t].wait()
        for h in range(groups * heads):
            own_kv[h, t] = flat_vm[t, :, h * D:(h + 1) * D]

    partners = heads - 1
    for o in range(1, REACH + 1):
        partners = partners + jnp.where(has_next[o], 1, 0) + jnp.where(has_prev[o], 1, 0)
    pl.semaphore_wait(barrier, partners)

    for g in range(groups):
        for j in range(1, heads):
            across(g, j).start()
        for o in range(REACH, 0, -1):
            @pl.when(sends(g, o))
            def _():
                onward(g, 0, o).start()

    for g in range(groups):
        for t in range(2):
            kv[0, g, t, rows(me)] = own_kv[me * groups + g, t]
    for o in range(1, REACH + 1):
        @pl.when(jnp.logical_not(has_prev[o]))
        def _():
            kv[o] = jnp.zeros(kv.shape[1:], kv.dtype)

        @pl.when(jnp.logical_not(has_next[o]))
        def _():
            got[o - 1] = jnp.zeros(got.shape[1:], got.dtype)

    if last > 0:
        @pl.when(odd_next)
        def _():
            got[1, :last] = jnp.zeros((last,) + got.shape[2:], got.dtype)

    seg_copy.wait()

    def seg_row(o):
        row = seg_vm[pl.ds(jnp.maximum(shard - o, 0), 1), :]
        return jnp.where(shard >= o, row, -1)

    def tall(row):
        return jnp.transpose(jnp.broadcast_to(row, (length, length)))

    seg_here = seg_row(0)
    key_index = lax.broadcasted_iota(jnp.int32, (length, length), 0)
    query_index = lax.broadcasted_iota(jnp.int32, (length, length), 1)
    lower = key_index <= query_index
    merged = jnp.where(lower, tall(seg_here), tall(seg_row(2)))
    blocked = -jnp.inf
    bias_own = jnp.where(merged == seg_here, 0.0, blocked)
    bias_prev = jnp.where(tall(seg_row(1)) == seg_here, 0.0, blocked)
    one_low = jnp.where(lower, 1.0, 0.0).astype(jnp.bfloat16)
    for i in range(PAIR):
        bias[0, :, i * D:(i + 1) * D] = bias_own
        bias[1, :, i * D:(i + 1) * D] = bias_prev
        low[:, i * D:(i + 1) * D] = one_low

    for g in range(groups):
        for j in range(1, heads):
            across(g, j).wait_recv()
            for o in range(REACH, 0, -1):
                @pl.when(sends(g, o))
                def _():
                    onward(g, j, o).start()

    wide_lower = lax.broadcasted_iota(jnp.int32, (length, lanes), 0) <= lax.rem(
        lax.broadcasted_iota(jnp.int32, (length, lanes), 1), D
    )

    def merge(g):
        back_near(g).wait_recv()
        stage[0, g] = (hold[g] + mid[g].astype(jnp.float32)).astype(jnp.bfloat16)
        back(g, 1).start()

    def one_group(g, carry):
        for t in range(2):
            load(g, t).wait()
        for o in range(1, REACH + 1):
            fresh = has_prev[o]
            if o == 1:
                fresh = jnp.logical_and(
                    fresh, jnp.logical_or(g == 0, jnp.logical_not(relays))
                )

            @pl.when(fresh)
            def _():
                onward_all(g, o).wait_recv()

        keys = jnp.concatenate([kv[o, g, 0] for o in ORDER], 0)
        values = jnp.concatenate([kv[o, g, 1] for o in ORDER], 0)
        heads_q = []
        first_q = g * qw
        for u in range(GROUP // PAIR):
            spans = [cols(first_q + u * lanes + i * D, D) for i in range(PAIR)]
            q = jnp.concatenate([q_vm[:, s] for s in spans], 0)
            do = jnp.concatenate([do_vm[:, s] for s in spans], 0)
            heads_q.append((q, do, nt(keys, q), nt(values, do)))
        unit = scale * math.log2(math.e)
        for u, (q, do, scores, d_w) in enumerate(heads_q):
            s_own = jnp.where(wide_lower, scores[:length], scores[length:2 * length]) + bias[0]
            s_prev = scores[2 * length:] + bias[1]
            top = jnp.maximum(
                jnp.max(s_own, 0, keepdims=True), jnp.max(s_prev, 0, keepdims=True)
            )
            e_own = jnp.exp2((s_own - top) * unit)
            e_prev = jnp.exp2((s_prev - top) * unit)
            inv = 1.0 / (
                jnp.sum(e_own, 0, keepdims=True) + jnp.sum(e_prev, 0, keepdims=True)
            )
            w_own = e_own * inv
            w_prev = e_prev * inv
            d_own = jnp.where(wide_lower, d_w[:length], d_w[length:2 * length])
            d_prev = d_w[2 * length:]
            delta = jnp.sum(w_own * d_own, 0, keepdims=True) + jnp.sum(
                w_prev * d_prev, 0, keepdims=True
            )
            r_own = w_own.astype(jnp.bfloat16)
            g_own = (w_own * (d_own - delta)).astype(jnp.bfloat16)
            keep = low[...]
            r_low = r_own * keep
            g_low = g_own * keep
            lane = slice(u * lanes, (u + 1) * lanes)
            w_vm[g, :length, lane] = r_low
            w_vm[g, length:2 * length, lane] = r_own - r_low
            w_vm[g, 2 * length:, lane] = w_prev.astype(jnp.bfloat16)
            ds_vm[g, :length, lane] = g_low
            ds_vm[g, length:2 * length, lane] = g_own - g_low
            ds_vm[g, 2 * length:, lane] = (w_prev * (d_prev - delta)).astype(jnp.bfloat16)
        @pl.when(jnp.logical_and(relays, g < last))
        def _():
            onward_all(g + 1, 1).wait_recv()
            relay(g + 1).start()

        dk_sum = nn(ds_vm[g], jnp.concatenate([h[0] for h in heads_q], 0))
        dv_sum = nn(w_vm[g], jnp.concatenate([h[1] for h in heads_q], 0))
        for t, total in enumerate((dk_sum * scale, dv_sum)):
            for at, o in enumerate(ORDER):
                block = total[at * length:(at + 1) * length]
                if o == 0:
                    own[g, t] = block
                elif o == 1:
                    hold[g, t] = block
                else:
                    stage[1, g, t] = block.astype(jnp.bfloat16)

        @pl.when(has_prev[2])
        def _():
            @pl.when(jnp.logical_or(even, g == last))
            def _():
                back(g, 2).start()

            @pl.when(jnp.logical_and(odd, g < last))
            def _():
                back_near(g).start()

        @pl.when(jnp.logical_or(odd, jnp.logical_and(relays, g == last)))
        def _():
            stage[0, g] = hold[g].astype(jnp.bfloat16)
            back(g, 1).start()

        @pl.when(jnp.logical_and(relays, g >= 1))
        def _():
            merge(g - 1)

        return carry

    lax.fori_loop(0, groups, one_group, 0)
    lax.fori_loop(
        0, groups // 2, functools.partial(outputs, kv, w_vm, ds_vm, att_ref, dq_ref, 0), 0
    )

    for g in range(groups):
        for o in range(1, REACH + 1):
            @pl.when(has_next[o] if o == 1 or g == last else even_next)
            def _():
                back(g, o).wait_recv()
        total = own[g]
        for o in range(1, REACH + 1):
            total = total + got[o - 1, g].astype(jnp.float32)
        final[g] = total.astype(jnp.bfloat16)
        for j in range(1, heads):
            home(g, j).start()
        dkv_ref[me * groups + g] = final[g, :, rows(me)]

    for j in range(1, heads):
        share = own_kv.at[pl.ds(0, groups)]
        remote(share, share, y_send.at[j - 1], y_recv.at[j - 1, 0], at_head(after(j))).wait_send()
        landed = dkv_ref.at[pl.ds(0, groups)]
        ends = remote(share, landed, z_send.at[j - 1], z_recv.at[j - 1], at_head(after(j)))
        ends.wait_send()
        ends.wait_recv()
    def sent(o, block):
        remote(
            kv.at[0, block], kv.at[o, block], f_send.at[o - 1], f_recv.at[o - 1, 0],
            at_shard(shard + o),
        ).wait_send()

    @pl.when(has_next[1])
    def _():
        sent(1, pl.ds(0, groups))

    @pl.when(even_next)
    def _():
        sent(2, pl.ds(0, groups))

    @pl.when(odd_next)
    def _():
        sent(2, pl.ds(0, 1))

    for o in range(1, REACH + 1):
        @pl.when(has_prev[o])
        def _():
            remote(
                stage.at[o - 1], got.at[o - 1], b_send.at[o - 1], b_recv.at[o - 1, 0],
                at_shard(shard - o),
            ).wait_send()

    if last > 0:
        @pl.when(relays)
        def _():
            block = pl.ds(1, last)
            remote(
                kv.at[1, block], kv.at[2, block], r_send, f_recv.at[1, 0], at_shard(shard + 1)
            ).wait_send()


def finish(
    att_a, dq_a, dkv, w_vm, ds_vm, kv, att_out, dq_out, dk_out, dv_out,
    att_b, dq_b, flat, sems, late
):
    groups = w_vm.shape[0]
    half = groups // 2
    qw = GROUP * HEAD_SIZE
    early = pl.ds(0, half * qw)
    copies = []
    for i, (src, dst) in enumerate((
        (att_a, att_out.at[:, early]), (dq_a, dq_out.at[:, early]),
        (flat.at[0], dk_out), (flat.at[1], dv_out),
    )):
        if i >= 2:
            for h in range(dkv.shape[0]):
                flat[i - 2, :, h * HEAD_SIZE:(h + 1) * HEAD_SIZE] = dkv[h, i - 2]
        copies.append(pltpu.make_async_copy(src, dst, sems.at[i]))
        copies[-1].start()

    for g in range(half, groups):
        outputs(kv, w_vm, ds_vm, att_b, dq_b, half, g, 0)
        here, there = pl.ds((g - half) * qw, qw), pl.ds(g * qw, qw)
        for t, (src, dst) in enumerate(((att_b, att_out), (dq_b, dq_out))):
            copies.append(
                pltpu.make_async_copy(src.at[:, here], dst.at[:, there], late.at[t, g - half])
            )
            copies[-1].start()
    for copy in copies:
        copy.wait()


def body(mesh, query, key, value, output_cotangent, segment):
    length, wide = query.shape
    part, kv_wide = key.shape
    heads = mesh.shape["head"]
    inners = mesh.shape["inner"]
    shards = mesh.shape["outer"] * inners
    groups = kv_wide // heads // HEAD_SIZE
    bf, f32 = jnp.bfloat16, jnp.float32
    dma = pltpu.SemaphoreType.DMA
    peers = max(heads - 1, 1)
    lanes = PAIR * HEAD_SIZE
    shapes = ((length, wide), (length, wide), (part, kv_wide), (part, kv_wide))
    half = groups // 2
    qw = GROUP * HEAD_SIZE
    block = (groups, 2, length, HEAD_SIZE)
    made = (groups, (REACH + 1) * length, qw)
    passed = (
        (length, half * qw), (length, half * qw), (groups * heads, 2, part, HEAD_SIZE),
        made, made, (REACH + 1, groups, 2, length, HEAD_SIZE),
    )
    operands = (query, key, value, output_cotangent, segment.reshape(shards, length))
    results = pl.pallas_call(
        functools.partial(kernel, inners, shards, heads),
        out_shape=tuple(pltpu.VMEM(shape, bf) for shape in passed),
        in_specs=[pl.BlockSpec(memory_space=pltpu.HBM)] * 5,
        out_specs=[pl.BlockSpec(memory_space=pltpu.VMEM)] * len(passed),
        scratch_shapes=[
            pltpu.VMEM((length, wide), bf),
            pltpu.VMEM((length, wide), bf),
            pltpu.VMEM((shards, length), jnp.int32),
            pltpu.VMEM((2, part, kv_wide), bf),
            pltpu.VMEM((groups * heads, 2, part, HEAD_SIZE), bf),
            pltpu.VMEM(block, f32),
            pltpu.VMEM(block, f32),
            pltpu.VMEM(block, bf),
            pltpu.VMEM((REACH,) + block, bf),
            pltpu.VMEM((REACH,) + block, bf),
            pltpu.VMEM(block, bf),
            pltpu.VMEM((2, length, lanes), f32),
            pltpu.VMEM((length, lanes), bf),
            dma((2, groups)),
            dma(()),
            dma((2,)),
            dma((peers,)),
            dma((peers, groups)),
            dma((REACH,)),
            dma((REACH, groups)),
            dma(()),
            dma((groups,)),
            dma((REACH,)),
            dma((REACH, groups)),
            dma((peers,)),
            dma((peers,)),
        ],
        compiler_params=pltpu.CompilerParams(
            collective_id=0, has_side_effects=True, vmem_limit_bytes=40 * 2**20
        ),
        name="packed_attention",
    )(*(pltpu.with_memory_space_constraint(x, pltpu.HBM) for x in operands))
    return pl.pallas_call(
        finish,
        out_shape=tuple(jax.ShapeDtypeStruct(shape, bf) for shape in shapes),
        in_specs=[pl.BlockSpec(memory_space=pltpu.VMEM)] * len(passed),
        out_specs=[pl.BlockSpec(memory_space=pltpu.HBM)] * 4,
        scratch_shapes=[
            pltpu.VMEM((length, wide - half * qw), bf),
            pltpu.VMEM((length, wide - half * qw), bf),
            pltpu.VMEM((2, part, kv_wide), bf),
            dma((4,)),
            dma((2, groups - half)),
        ],
        compiler_params=pltpu.CompilerParams(vmem_limit_bytes=16 * 2**20),
        name="finish",
    )(*results)


def solution(mesh):
    in_specs = (
        P(("outer", "inner"), "head"),
        P(("outer", "inner", "head"), None),
        P(("outer", "inner", "head"), None),
        P(("outer", "inner"), "head"),
        P(),
    )
    out_specs = (
        P(("outer", "inner"), "head"),
        P(("outer", "inner"), "head"),
        P(("outer", "inner", "head"), None),
        P(("outer", "inner", "head"), None),
    )
    return jax.shard_map(
        functools.partial(body, mesh),
        mesh=mesh, in_specs=in_specs, out_specs=out_specs, check_vma=False,
    )
```

```python
import functools
import math

import jax
import jax.numpy as jnp
from jax import lax
from jax.experimental import pallas as pl
from jax.experimental.pallas import tpu as pltpu
from jax.sharding import PartitionSpec as P

QUERY_HEADS = 48
KEY_VALUE_HEADS = 8
HEAD_SIZE = 128
REACH = 2
GROUP = QUERY_HEADS // KEY_VALUE_HEADS
PAIR = 2
MESH = pl.DeviceIdType.MESH


def nt(a, b):
    return lax.dot_general(a, b, (((1,), (1,)), ((), ())), preferred_element_type=jnp.float32)


def tn(a, b):
    return lax.dot_general(a, b, (((0,), (0,)), ((), ())), preferred_element_type=jnp.float32)


def nn(a, b):
    return lax.dot_general(a, b, (((1,), (0,)), ((), ())), preferred_element_type=jnp.float32)


ORDER = (0, 2, 1)


def outputs(kv, w_vm, ds_vm, att, dq, base, g, carry):
    D = HEAD_SIZE
    length = kv.shape[3]
    lanes = PAIR * D
    for t, src, dst, by in ((1, w_vm, att, None), (0, ds_vm, dq, 1.0 / math.sqrt(D))):
        flat = jnp.transpose(jnp.concatenate([kv[o, g, t] for o in ORDER], 0))
        for u in range(GROUP // PAIR):
            made = nn(flat, src[g, :, u * lanes:(u + 1) * lanes])
            if by is not None:
                made = made * by
            made = jnp.transpose(made.astype(jnp.bfloat16))
            for i in range(PAIR):
                start = (g - base) * GROUP * D + u * lanes + i * D
                dst[:, pl.ds(pl.multiple_of(start, D), D)] = made[i * length:(i + 1) * length]
    return carry


def kernel(
    inners, shards, heads,
    query_ref, key_ref, value_ref, cot_ref, seg_ref,
    att_ref, dq_ref, dkv_ref, w_vm, ds_vm, kv,
    q_vm, do_vm, seg_vm, flat_vm, own_kv, own, hold, mid, stage, got, final, bias, low,
    in_sem, seg_sem, kv_sem,
    y_send, y_recv, f_send, f_recv, r_send, m_recv, b_send, b_recv, z_send, z_recv,
):
    D = HEAD_SIZE
    length = q_vm.shape[0]
    groups = kv.shape[1]
    part = length // heads
    qw = GROUP * D
    lanes = PAIR * D
    scale = 1.0 / math.sqrt(D)
    shard = lax.axis_index("outer") * inners + lax.axis_index("inner")
    me = lax.axis_index("head")

    def at_shard(target):
        return {"outer": lax.div(target, inners), "inner": lax.rem(target, inners), "head": me}

    def at_head(target):
        return {"head": target}

    def rows(p):
        return pl.ds(pl.multiple_of(p * part, part), part)

    def cols(start, size):
        return pl.ds(pl.multiple_of(start, D), size)

    def before(j):
        return lax.rem(me + heads - j, heads)

    def after(j):
        return lax.rem(me + j, heads)

    def remote(src, dst, send, recv, target):
        return pltpu.make_async_remote_copy(
            src_ref=src, dst_ref=dst, send_sem=send, recv_sem=recv,
            device_id=target, device_id_type=MESH,
        )

    def load(g, which):
        src, dst = ((query_ref, q_vm), (cot_ref, do_vm))[which]
        c = cols(g * qw, qw)
        return pltpu.make_async_copy(src.at[:, c], dst.at[:, c], in_sem.at[which, g])

    def across(g, j):
        return remote(
            own_kv.at[after(j) * groups + g], kv.at[0, g, :, rows(me)],
            y_send.at[j - 1], y_recv.at[j - 1, g], at_head(after(j)),
        )

    def onward(g, j, o):
        r = rows(before(j))
        src = own_kv.at[me * groups + g] if j == 0 else kv.at[0, g, :, r]
        return remote(
            src, kv.at[o, g, :, r], f_send.at[o - 1], f_recv.at[o - 1, g], at_shard(shard + o)
        )

    def onward_all(g, o):
        return remote(
            kv.at[0, g], kv.at[o, g], f_send.at[o - 1], f_recv.at[o - 1, g], at_shard(shard + o)
        )

    def relay(g):
        return remote(
            kv.at[1, g], kv.at[2, g], r_send, f_recv.at[1, g], at_shard(shard + 1)
        )

    def back_near(g):
        return remote(stage.at[1, g], mid.at[g], b_send.at[1], m_recv.at[g], at_shard(shard - 1))

    def back(g, o):
        return remote(
            stage.at[o - 1, g], got.at[o - 1, g], b_send.at[o - 1], b_recv.at[o - 1, g],
            at_shard(shard - o),
        )

    def home(g, j):
        return remote(
            final.at[g, :, rows(after(j))], dkv_ref.at[me * groups + g],
            z_send.at[j - 1], z_recv.at[j - 1], at_head(after(j)),
        )

    has_next = [None] + [shard + o < shards for o in range(1, REACH + 1)]
    has_prev = [None] + [shard >= o for o in range(1, REACH + 1)]

    even = lax.rem(shard, 2) == 0
    odd = jnp.logical_not(even)
    deals_next = [None, has_next[1], jnp.logical_and(even, has_next[2])]
    deals_prev = [None, has_prev[1], jnp.logical_and(even, has_prev[2])]
    relays = deals_prev[2]

    barrier = pltpu.get_barrier_semaphore()
    for j in range(1, heads):
        pl.semaphore_signal(barrier, inc=1, device_id=at_head(after(j)), device_id_type=MESH)
    for o in range(1, REACH + 1):
        @pl.when(deals_next[o])
        def _():
            pl.semaphore_signal(barrier, inc=1, device_id=at_shard(shard + o), device_id_type=MESH)

        @pl.when(deals_prev[o])
        def _():
            pl.semaphore_signal(barrier, inc=1, device_id=at_shard(shard - o), device_id_type=MESH)

    kv_loads = [
        pltpu.make_async_copy(ref, flat_vm.at[t], kv_sem.at[t])
        for t, ref in enumerate((key_ref, value_ref))
    ]
    for copy in kv_loads:
        copy.start()
    seg_copy = pltpu.make_async_copy(seg_ref, seg_vm, seg_sem)
    seg_copy.start()
    for g in range(groups):
        for t in range(2):
            load(g, t).start()

    for t in range(2):
        kv_loads[t].wait()
        for h in range(groups * heads):
            own_kv[h, t] = flat_vm[t, :, h * D:(h + 1) * D]

    partners = heads - 1
    for o in range(1, REACH + 1):
        partners = partners + jnp.where(deals_next[o], 1, 0) + jnp.where(deals_prev[o], 1, 0)
    pl.semaphore_wait(barrier, partners)

    def share(g):
        if g < groups:
            for j in range(1, heads):
                across(g, j).start()

    def pass_own(g):
        if g < groups:
            for o in range(REACH, 0, -1):
                @pl.when(deals_next[o])
                def _():
                    onward(g, 0, o).start()

    share(0)
    pass_own(0)
    share(1)

    for g in range(groups):
        for t in range(2):
            kv[0, g, t, rows(me)] = own_kv[me * groups + g, t]
    for o in range(1, REACH + 1):
        @pl.when(jnp.logical_not(has_prev[o]))
        def _():
            kv[o] = jnp.zeros(kv.shape[1:], kv.dtype)

        @pl.when(jnp.logical_not(deals_next[o]))
        def _():
            got[o - 1] = jnp.zeros(got.shape[1:], got.dtype)

    seg_copy.wait()

    def seg_row(o):
        row = seg_vm[pl.ds(jnp.maximum(shard - o, 0), 1), :]
        return jnp.where(shard >= o, row, -1)

    def tall(row):
        return jnp.transpose(jnp.broadcast_to(row, (length, length)))

    seg_here = seg_row(0)
    key_index = lax.broadcasted_iota(jnp.int32, (length, length), 0)
    query_index = lax.broadcasted_iota(jnp.int32, (length, length), 1)
    lower = key_index <= query_index
    merged = jnp.where(lower, tall(seg_here), tall(seg_row(2)))
    blocked = -jnp.inf
    bias_own = jnp.where(merged == seg_here, 0.0, blocked)
    bias_prev = jnp.where(tall(seg_row(1)) == seg_here, 0.0, blocked)
    one_low = jnp.where(lower, 1.0, 0.0).astype(jnp.bfloat16)
    for i in range(PAIR):
        bias[0, :, i * D:(i + 1) * D] = bias_own
        bias[1, :, i * D:(i + 1) * D] = bias_prev
        low[:, i * D:(i + 1) * D] = one_low

    for g in range(groups):
        for j in range(1, heads):
            across(g, j).wait_recv()
            for o in range(REACH, 0, -1):
                @pl.when(deals_next[o])
                def _():
                    onward(g, j, o).start()
        share(g + 2)
        pass_own(g + 1)

    wide_lower = lax.broadcasted_iota(jnp.int32, (length, lanes), 0) <= lax.rem(
        lax.broadcasted_iota(jnp.int32, (length, lanes), 1), D
    )

    def merge(g):
        back_near(g).wait_recv()
        stage[0, g] = (hold[g] + mid[g].astype(jnp.float32)).astype(jnp.bfloat16)
        back(g, 1).start()

    def one_group(g, carry):
        for t in range(2):
            load(g, t).wait()
        for o in range(1, REACH + 1):
            @pl.when(has_prev[o])
            def _():
                onward_all(g, o).wait_recv()

            if o == 1:
                @pl.when(relays)
                def _():
                    relay(g).start()
        keys = jnp.concatenate([kv[o, g, 0] for o in ORDER], 0)
        values = jnp.concatenate([kv[o, g, 1] for o in ORDER], 0)
        heads_q = []
        first_q = g * qw
        for u in range(GROUP // PAIR):
            spans = [cols(first_q + u * lanes + i * D, D) for i in range(PAIR)]
            q = jnp.concatenate([q_vm[:, s] for s in spans], 0)
            do = jnp.concatenate([do_vm[:, s] for s in spans], 0)
            heads_q.append((q, do, nt(keys, q), nt(values, do)))
        unit = scale * math.log2(math.e)
        for u, (q, do, scores, d_w) in enumerate(heads_q):
            s_own = jnp.where(wide_lower, scores[:length], scores[length:2 * length]) + bias[0]
            s_prev = scores[2 * length:] + bias[1]
            top = jnp.maximum(
                jnp.max(s_own, 0, keepdims=True), jnp.max(s_prev, 0, keepdims=True)
            )
            e_own = jnp.exp2((s_own - top) * unit)
            e_prev = jnp.exp2((s_prev - top) * unit)
            inv = 1.0 / (
                jnp.sum(e_own, 0, keepdims=True) + jnp.sum(e_prev, 0, keepdims=True)
            )
            w_own = e_own * inv
            w_prev = e_prev * inv
            d_own = jnp.where(wide_lower, d_w[:length], d_w[length:2 * length])
            d_prev = d_w[2 * length:]
            delta = jnp.sum(w_own * d_own, 0, keepdims=True) + jnp.sum(
                w_prev * d_prev, 0, keepdims=True
            )
            r_own = w_own.astype(jnp.bfloat16)
            g_own = (w_own * (d_own - delta)).astype(jnp.bfloat16)
            keep = low[...]
            r_low = r_own * keep
            g_low = g_own * keep
            lane = slice(u * lanes, (u + 1) * lanes)
            w_vm[g, :length, lane] = r_low
            w_vm[g, length:2 * length, lane] = r_own - r_low
            w_vm[g, 2 * length:, lane] = w_prev.astype(jnp.bfloat16)
            ds_vm[g, :length, lane] = g_low
            ds_vm[g, length:2 * length, lane] = g_own - g_low
            ds_vm[g, 2 * length:, lane] = (w_prev * (d_prev - delta)).astype(jnp.bfloat16)
        dk_sum = nn(ds_vm[g], jnp.concatenate([h[0] for h in heads_q], 0))
        dv_sum = nn(w_vm[g], jnp.concatenate([h[1] for h in heads_q], 0))
        for t, total in enumerate((dk_sum * scale, dv_sum)):
            for at, o in enumerate(ORDER):
                block = total[at * length:(at + 1) * length]
                if o == 0:
                    own[g, t] = block
                elif o == 1:
                    hold[g, t] = block
                else:
                    stage[1, g, t] = block.astype(jnp.bfloat16)

        @pl.when(relays)
        def _():
            back(g, 2).start()

            @pl.when(g >= 1)
            def _():
                merge(g - 1)

        @pl.when(jnp.logical_and(odd, has_prev[2]))
        def _():
            back_near(g).start()

        @pl.when(odd)
        def _():
            stage[0, g] = hold[g].astype(jnp.bfloat16)
            back(g, 1).start()

        return carry

    lax.fori_loop(0, groups, one_group, 0)
    lax.fori_loop(
        0, groups // 2, functools.partial(outputs, kv, w_vm, ds_vm, att_ref, dq_ref, 0), 0
    )

    @pl.when(relays)
    def _():
        merge(groups - 1)

    for g in range(groups):
        for o in range(1, REACH + 1):
            @pl.when(deals_next[o])
            def _():
                back(g, o).wait_recv()
        total = own[g]
        for o in range(1, REACH + 1):
            total = total + got[o - 1, g].astype(jnp.float32)
        final[g] = total.astype(jnp.bfloat16)
        for j in range(1, heads):
            home(g, j).start()
        dkv_ref[me * groups + g] = final[g, :, rows(me)]

    for j in range(1, heads):
        share = own_kv.at[pl.ds(0, groups)]
        remote(share, share, y_send.at[j - 1], y_recv.at[j - 1, 0], at_head(after(j))).wait_send()
        landed = dkv_ref.at[pl.ds(0, groups)]
        ends = remote(share, landed, z_send.at[j - 1], z_recv.at[j - 1], at_head(after(j)))
        ends.wait_send()
        ends.wait_recv()
    for o in range(1, REACH + 1):
        @pl.when(deals_next[o])
        def _():
            remote(
                kv.at[0], kv.at[o], f_send.at[o - 1], f_recv.at[o - 1, 0], at_shard(shard + o)
            ).wait_send()

        @pl.when(has_prev[o])
        def _():
            remote(
                stage.at[o - 1], got.at[o - 1], b_send.at[o - 1], b_recv.at[o - 1, 0],
                at_shard(shard - o),
            ).wait_send()

    @pl.when(relays)
    def _():
        remote(kv.at[1], kv.at[2], r_send, f_recv.at[1, 0], at_shard(shard + 1)).wait_send()


def finish(
    att_a, dq_a, dkv, w_vm, ds_vm, kv, att_out, dq_out, dk_out, dv_out,
    att_b, dq_b, flat, sems, late
):
    groups = w_vm.shape[0]
    half = groups // 2
    qw = GROUP * HEAD_SIZE
    early = pl.ds(0, half * qw)
    copies = []
    for i, (src, dst) in enumerate((
        (att_a, att_out.at[:, early]), (dq_a, dq_out.at[:, early]),
        (flat.at[0], dk_out), (flat.at[1], dv_out),
    )):
        if i >= 2:
            for h in range(dkv.shape[0]):
                flat[i - 2, :, h * HEAD_SIZE:(h + 1) * HEAD_SIZE] = dkv[h, i - 2]
        copies.append(pltpu.make_async_copy(src, dst, sems.at[i]))
        copies[-1].start()

    for g in range(half, groups):
        outputs(kv, w_vm, ds_vm, att_b, dq_b, half, g, 0)
        here, there = pl.ds((g - half) * qw, qw), pl.ds(g * qw, qw)
        for t, (src, dst) in enumerate(((att_b, att_out), (dq_b, dq_out))):
            copies.append(
                pltpu.make_async_copy(src.at[:, here], dst.at[:, there], late.at[t, g - half])
            )
            copies[-1].start()
    for copy in copies:
        copy.wait()


def body(mesh, query, key, value, output_cotangent, segment):
    length, wide = query.shape
    part, kv_wide = key.shape
    heads = mesh.shape["head"]
    inners = mesh.shape["inner"]
    shards = mesh.shape["outer"] * inners
    groups = kv_wide // heads // HEAD_SIZE
    bf, f32 = jnp.bfloat16, jnp.float32
    dma = pltpu.SemaphoreType.DMA
    peers = max(heads - 1, 1)
    lanes = PAIR * HEAD_SIZE
    shapes = ((length, wide), (length, wide), (part, kv_wide), (part, kv_wide))
    half = groups // 2
    qw = GROUP * HEAD_SIZE
    block = (groups, 2, length, HEAD_SIZE)
    made = (groups, (REACH + 1) * length, qw)
    passed = (
        (length, half * qw), (length, half * qw), (groups * heads, 2, part, HEAD_SIZE),
        made, made, (REACH + 1, groups, 2, length, HEAD_SIZE),
    )
    operands = (query, key, value, output_cotangent, segment.reshape(shards, length))
    results = pl.pallas_call(
        functools.partial(kernel, inners, shards, heads),
        out_shape=tuple(pltpu.VMEM(shape, bf) for shape in passed),
        in_specs=[pl.BlockSpec(memory_space=pltpu.HBM)] * 5,
        out_specs=[pl.BlockSpec(memory_space=pltpu.VMEM)] * len(passed),
        scratch_shapes=[
            pltpu.VMEM((length, wide), bf),
            pltpu.VMEM((length, wide), bf),
            pltpu.VMEM((shards, length), jnp.int32),
            pltpu.VMEM((2, part, kv_wide), bf),
            pltpu.VMEM((groups * heads, 2, part, HEAD_SIZE), bf),
            pltpu.VMEM(block, f32),
            pltpu.VMEM(block, f32),
            pltpu.VMEM(block, bf),
            pltpu.VMEM((REACH,) + block, bf),
            pltpu.VMEM((REACH,) + block, bf),
            pltpu.VMEM(block, bf),
            pltpu.VMEM((2, length, lanes), f32),
            pltpu.VMEM((length, lanes), bf),
            dma((2, groups)),
            dma(()),
            dma((2,)),
            dma((peers,)),
            dma((peers, groups)),
            dma((REACH,)),
            dma((REACH, groups)),
            dma(()),
            dma((groups,)),
            dma((REACH,)),
            dma((REACH, groups)),
            dma((peers,)),
            dma((peers,)),
        ],
        compiler_params=pltpu.CompilerParams(
            collective_id=0, has_side_effects=True, vmem_limit_bytes=40 * 2**20
        ),
        name="packed_attention",
    )(*(pltpu.with_memory_space_constraint(x, pltpu.HBM) for x in operands))
    return pl.pallas_call(
        finish,
        out_shape=tuple(jax.ShapeDtypeStruct(shape, bf) for shape in shapes),
        in_specs=[pl.BlockSpec(memory_space=pltpu.VMEM)] * len(passed),
        out_specs=[pl.BlockSpec(memory_space=pltpu.HBM)] * 4,
        scratch_shapes=[
            pltpu.VMEM((length, wide - half * qw), bf),
            pltpu.VMEM((length, wide - half * qw), bf),
            pltpu.VMEM((2, part, kv_wide), bf),
            dma((4,)),
            dma((2, groups - half)),
        ],
        compiler_params=pltpu.CompilerParams(vmem_limit_bytes=16 * 2**20),
        name="finish",
    )(*results)


def solution(mesh):
    in_specs = (
        P(("outer", "inner"), "head"),
        P(("outer", "inner", "head"), None),
        P(("outer", "inner", "head"), None),
        P(("outer", "inner"), "head"),
        P(),
    )
    out_specs = (
        P(("outer", "inner"), "head"),
        P(("outer", "inner"), "head"),
        P(("outer", "inner", "head"), None),
        P(("outer", "inner", "head"), None),
    )
    return jax.shard_map(
        functools.partial(body, mesh),
        mesh=mesh, in_specs=in_specs, out_specs=out_specs, check_vma=False,
    )
```

```python
import functools
import math

import jax
import jax.numpy as jnp
from jax import lax
from jax.experimental import pallas as pl
from jax.experimental.pallas import tpu as pltpu
from jax.sharding import PartitionSpec as P

QUERY_HEADS = 48
KEY_VALUE_HEADS = 8
HEAD_SIZE = 128
REACH = 2
GROUP = QUERY_HEADS // KEY_VALUE_HEADS
PAIR = 2
MESH = pl.DeviceIdType.MESH


def nt(a, b):
    return lax.dot_general(a, b, (((1,), (1,)), ((), ())), preferred_element_type=jnp.float32)


def tn(a, b):
    return lax.dot_general(a, b, (((0,), (0,)), ((), ())), preferred_element_type=jnp.float32)


def nn(a, b):
    return lax.dot_general(a, b, (((1,), (0,)), ((), ())), preferred_element_type=jnp.float32)


ORDER = (0, 2, 1)


def outputs(kv, w_vm, ds_vm, att, dq, base, g, carry):
    D = HEAD_SIZE
    length = kv.shape[3]
    lanes = PAIR * D
    for t, src, dst, by in ((1, w_vm, att, None), (0, ds_vm, dq, 1.0 / math.sqrt(D))):
        flat = jnp.transpose(jnp.concatenate([kv[o, g, t] for o in ORDER], 0))
        for u in range(GROUP // PAIR):
            made = nn(flat, src[g, :, u * lanes:(u + 1) * lanes])
            if by is not None:
                made = made * by
            made = jnp.transpose(made.astype(jnp.bfloat16))
            for i in range(PAIR):
                start = (g - base) * GROUP * D + u * lanes + i * D
                dst[:, pl.ds(pl.multiple_of(start, D), D)] = made[i * length:(i + 1) * length]
    return carry


def kernel(
    inners, shards, heads,
    query_ref, key_ref, value_ref, cot_ref, seg_ref,
    att_ref, dq_ref, dkv_ref, w_vm, ds_vm, kv,
    q_vm, do_vm, seg_vm, flat_vm, own_kv, own, hold, mid, stage, got, final, bias, low,
    in_sem, seg_sem, kv_sem,
    y_send, y_recv, f_send, f_recv, r_send, m_recv, b_send, b_recv, z_send, z_recv,
):
    D = HEAD_SIZE
    length = q_vm.shape[0]
    groups = kv.shape[1]
    part = length // heads
    qw = GROUP * D
    lanes = PAIR * D
    scale = 1.0 / math.sqrt(D)
    shard = lax.axis_index("outer") * inners + lax.axis_index("inner")
    me = lax.axis_index("head")

    def at_shard(target):
        return {"outer": lax.div(target, inners), "inner": lax.rem(target, inners), "head": me}

    def at_head(target):
        return {"head": target}

    def rows(p):
        return pl.ds(pl.multiple_of(p * part, part), part)

    def cols(start, size):
        return pl.ds(pl.multiple_of(start, D), size)

    def before(j):
        return lax.rem(me + heads - j, heads)

    def after(j):
        return lax.rem(me + j, heads)

    def remote(src, dst, send, recv, target):
        return pltpu.make_async_remote_copy(
            src_ref=src, dst_ref=dst, send_sem=send, recv_sem=recv,
            device_id=target, device_id_type=MESH,
        )

    def load(g, which):
        src, dst = ((query_ref, q_vm), (cot_ref, do_vm))[which]
        c = cols(g * qw, qw)
        return pltpu.make_async_copy(src.at[:, c], dst.at[:, c], in_sem.at[which, g])

    def across(g, j):
        return remote(
            own_kv.at[after(j) * groups + g], kv.at[0, g, :, rows(me)],
            y_send.at[j - 1], y_recv.at[j - 1, g], at_head(after(j)),
        )

    def onward(g, j, o):
        r = rows(before(j))
        src = own_kv.at[me * groups + g] if j == 0 else kv.at[0, g, :, r]
        return remote(
            src, kv.at[o, g, :, r], f_send.at[o - 1], f_recv.at[o - 1, g], at_shard(shard + o)
        )

    def onward_all(g, o):
        return remote(
            kv.at[0, g], kv.at[o, g], f_send.at[o - 1], f_recv.at[o - 1, g], at_shard(shard + o)
        )

    def relay(g):
        return remote(
            kv.at[1, g], kv.at[2, g], r_send, f_recv.at[1, g], at_shard(shard + 1)
        )

    def back_near(g):
        return remote(stage.at[1, g], mid.at[g], b_send.at[1], m_recv.at[g], at_shard(shard - 1))

    def back(g, o):
        return remote(
            stage.at[o - 1, g], got.at[o - 1, g], b_send.at[o - 1], b_recv.at[o - 1, g],
            at_shard(shard - o),
        )

    def home(g, j):
        return remote(
            final.at[g, :, rows(after(j))], dkv_ref.at[me * groups + g],
            z_send.at[j - 1], z_recv.at[j - 1], at_head(after(j)),
        )

    has_next = [None] + [shard + o < shards for o in range(1, REACH + 1)]
    has_prev = [None] + [shard >= o for o in range(1, REACH + 1)]

    even = lax.rem(shard, 2) == 0
    odd = jnp.logical_not(even)
    deals_next = [None, has_next[1], jnp.logical_and(even, has_next[2])]
    deals_prev = [None, has_prev[1], jnp.logical_and(even, has_prev[2])]
    relays = deals_prev[2]

    barrier = pltpu.get_barrier_semaphore()
    for j in range(1, heads):
        pl.semaphore_signal(barrier, inc=1, device_id=at_head(after(j)), device_id_type=MESH)
    for o in range(1, REACH + 1):
        @pl.when(deals_next[o])
        def _():
            pl.semaphore_signal(barrier, inc=1, device_id=at_shard(shard + o), device_id_type=MESH)

        @pl.when(deals_prev[o])
        def _():
            pl.semaphore_signal(barrier, inc=1, device_id=at_shard(shard - o), device_id_type=MESH)

    kv_loads = [
        pltpu.make_async_copy(ref, flat_vm.at[t], kv_sem.at[t])
        for t, ref in enumerate((key_ref, value_ref))
    ]
    for copy in kv_loads:
        copy.start()
    seg_copy = pltpu.make_async_copy(seg_ref, seg_vm, seg_sem)
    seg_copy.start()
    for g in range(groups):
        for t in range(2):
            load(g, t).start()

    for t in range(2):
        kv_loads[t].wait()
        for h in range(groups * heads):
            own_kv[h, t] = flat_vm[t, :, h * D:(h + 1) * D]

    partners = heads - 1
    for o in range(1, REACH + 1):
        partners = partners + jnp.where(deals_next[o], 1, 0) + jnp.where(deals_prev[o], 1, 0)
    pl.semaphore_wait(barrier, partners)

    def share(g):
        for j in range(1, heads):
            across(g, j).start()

    def pass_own(g):
        if g < groups:
            for o in range(REACH, 0, -1):
                @pl.when(deals_next[o])
                def _():
                    onward(g, 0, o).start()

    for g in range(groups):
        share(g)
        if g < 2:
            pass_own(g)

    for g in range(groups):
        for t in range(2):
            kv[0, g, t, rows(me)] = own_kv[me * groups + g, t]
    for o in range(1, REACH + 1):
        @pl.when(jnp.logical_not(has_prev[o]))
        def _():
            kv[o] = jnp.zeros(kv.shape[1:], kv.dtype)

        @pl.when(jnp.logical_not(deals_next[o]))
        def _():
            got[o - 1] = jnp.zeros(got.shape[1:], got.dtype)

    seg_copy.wait()

    def seg_row(o):
        row = seg_vm[pl.ds(jnp.maximum(shard - o, 0), 1), :]
        return jnp.where(shard >= o, row, -1)

    def tall(row):
        return jnp.transpose(jnp.broadcast_to(row, (length, length)))

    seg_here = seg_row(0)
    key_index = lax.broadcasted_iota(jnp.int32, (length, length), 0)
    query_index = lax.broadcasted_iota(jnp.int32, (length, length), 1)
    lower = key_index <= query_index
    merged = jnp.where(lower, tall(seg_here), tall(seg_row(2)))
    blocked = -jnp.inf
    bias_own = jnp.where(merged == seg_here, 0.0, blocked)
    bias_prev = jnp.where(tall(seg_row(1)) == seg_here, 0.0, blocked)
    one_low = jnp.where(lower, 1.0, 0.0).astype(jnp.bfloat16)
    for i in range(PAIR):
        bias[0, :, i * D:(i + 1) * D] = bias_own
        bias[1, :, i * D:(i + 1) * D] = bias_prev
        low[:, i * D:(i + 1) * D] = one_low

    for g in range(groups):
        for j in range(1, heads):
            across(g, j).wait_recv()
            for o in range(REACH, 0, -1):
                @pl.when(deals_next[o])
                def _():
                    onward(g, j, o).start()
        pass_own(g + 2)

    wide_lower = lax.broadcasted_iota(jnp.int32, (length, lanes), 0) <= lax.rem(
        lax.broadcasted_iota(jnp.int32, (length, lanes), 1), D
    )

    def merge(g):
        back_near(g).wait_recv()
        stage[0, g] = (hold[g] + mid[g].astype(jnp.float32)).astype(jnp.bfloat16)
        back(g, 1).start()

    def one_group(g, carry):
        for t in range(2):
            load(g, t).wait()
        for o in range(1, REACH + 1):
            @pl.when(has_prev[o])
            def _():
                onward_all(g, o).wait_recv()

            if o == 1:
                @pl.when(relays)
                def _():
                    relay(g).start()
        keys = jnp.concatenate([kv[o, g, 0] for o in ORDER], 0)
        values = jnp.concatenate([kv[o, g, 1] for o in ORDER], 0)
        heads_q = []
        first_q = g * qw
        for u in range(GROUP // PAIR):
            spans = [cols(first_q + u * lanes + i * D, D) for i in range(PAIR)]
            q = jnp.concatenate([q_vm[:, s] for s in spans], 0)
            do = jnp.concatenate([do_vm[:, s] for s in spans], 0)
            heads_q.append((q, do, nt(keys, q), nt(values, do)))
        unit = scale * math.log2(math.e)
        for u, (q, do, scores, d_w) in enumerate(heads_q):
            s_own = jnp.where(wide_lower, scores[:length], scores[length:2 * length]) + bias[0]
            s_prev = scores[2 * length:] + bias[1]
            top = jnp.maximum(
                jnp.max(s_own, 0, keepdims=True), jnp.max(s_prev, 0, keepdims=True)
            )
            e_own = jnp.exp2((s_own - top) * unit)
            e_prev = jnp.exp2((s_prev - top) * unit)
            inv = 1.0 / (
                jnp.sum(e_own, 0, keepdims=True) + jnp.sum(e_prev, 0, keepdims=True)
            )
            w_own = e_own * inv
            w_prev = e_prev * inv
            d_own = jnp.where(wide_lower, d_w[:length], d_w[length:2 * length])
            d_prev = d_w[2 * length:]
            delta = jnp.sum(w_own * d_own, 0, keepdims=True) + jnp.sum(
                w_prev * d_prev, 0, keepdims=True
            )
            r_own = w_own.astype(jnp.bfloat16)
            g_own = (w_own * (d_own - delta)).astype(jnp.bfloat16)
            keep = low[...]
            r_low = r_own * keep
            g_low = g_own * keep
            lane = slice(u * lanes, (u + 1) * lanes)
            w_vm[g, :length, lane] = r_low
            w_vm[g, length:2 * length, lane] = r_own - r_low
            w_vm[g, 2 * length:, lane] = w_prev.astype(jnp.bfloat16)
            ds_vm[g, :length, lane] = g_low
            ds_vm[g, length:2 * length, lane] = g_own - g_low
            ds_vm[g, 2 * length:, lane] = (w_prev * (d_prev - delta)).astype(jnp.bfloat16)
        dk_sum = nn(ds_vm[g], jnp.concatenate([h[0] for h in heads_q], 0))
        dv_sum = nn(w_vm[g], jnp.concatenate([h[1] for h in heads_q], 0))
        for t, total in enumerate((dk_sum * scale, dv_sum)):
            for at, o in enumerate(ORDER):
                block = total[at * length:(at + 1) * length]
                if o == 0:
                    own[g, t] = block
                elif o == 1:
                    hold[g, t] = block
                else:
                    stage[1, g, t] = block.astype(jnp.bfloat16)

        @pl.when(relays)
        def _():
            back(g, 2).start()

            @pl.when(g >= 1)
            def _():
                merge(g - 1)

        @pl.when(jnp.logical_and(odd, has_prev[2]))
        def _():
            back_near(g).start()

        @pl.when(odd)
        def _():
            stage[0, g] = hold[g].astype(jnp.bfloat16)
            back(g, 1).start()

        return carry

    lax.fori_loop(0, groups, one_group, 0)
    lax.fori_loop(
        0, groups // 2, functools.partial(outputs, kv, w_vm, ds_vm, att_ref, dq_ref, 0), 0
    )

    @pl.when(relays)
    def _():
        merge(groups - 1)

    for g in range(groups):
        for o in range(1, REACH + 1):
            @pl.when(deals_next[o])
            def _():
                back(g, o).wait_recv()
        total = own[g]
        for o in range(1, REACH + 1):
            total = total + got[o - 1, g].astype(jnp.float32)
        final[g] = total.astype(jnp.bfloat16)
        for j in range(1, heads):
            home(g, j).start()
        dkv_ref[me * groups + g] = final[g, :, rows(me)]

    for j in range(1, heads):
        share = own_kv.at[pl.ds(0, groups)]
        remote(share, share, y_send.at[j - 1], y_recv.at[j - 1, 0], at_head(after(j))).wait_send()
        landed = dkv_ref.at[pl.ds(0, groups)]
        ends = remote(share, landed, z_send.at[j - 1], z_recv.at[j - 1], at_head(after(j)))
        ends.wait_send()
        ends.wait_recv()
    for o in range(1, REACH + 1):
        @pl.when(deals_next[o])
        def _():
            remote(
                kv.at[0], kv.at[o], f_send.at[o - 1], f_recv.at[o - 1, 0], at_shard(shard + o)
            ).wait_send()

        @pl.when(has_prev[o])
        def _():
            remote(
                stage.at[o - 1], got.at[o - 1], b_send.at[o - 1], b_recv.at[o - 1, 0],
                at_shard(shard - o),
            ).wait_send()

    @pl.when(relays)
    def _():
        remote(kv.at[1], kv.at[2], r_send, f_recv.at[1, 0], at_shard(shard + 1)).wait_send()


def finish(
    att_a, dq_a, dkv, w_vm, ds_vm, kv, att_out, dq_out, dk_out, dv_out,
    att_b, dq_b, flat, sems, late
):
    groups = w_vm.shape[0]
    half = groups // 2
    qw = GROUP * HEAD_SIZE
    early = pl.ds(0, half * qw)
    copies = []
    for i, (src, dst) in enumerate((
        (att_a, att_out.at[:, early]), (dq_a, dq_out.at[:, early]),
        (flat.at[0], dk_out), (flat.at[1], dv_out),
    )):
        if i >= 2:
            for h in range(dkv.shape[0]):
                flat[i - 2, :, h * HEAD_SIZE:(h + 1) * HEAD_SIZE] = dkv[h, i - 2]
        copies.append(pltpu.make_async_copy(src, dst, sems.at[i]))
        copies[-1].start()

    for g in range(half, groups):
        outputs(kv, w_vm, ds_vm, att_b, dq_b, half, g, 0)
        here, there = pl.ds((g - half) * qw, qw), pl.ds(g * qw, qw)
        for t, (src, dst) in enumerate(((att_b, att_out), (dq_b, dq_out))):
            copies.append(
                pltpu.make_async_copy(src.at[:, here], dst.at[:, there], late.at[t, g - half])
            )
            copies[-1].start()
    for copy in copies:
        copy.wait()


def body(mesh, query, key, value, output_cotangent, segment):
    length, wide = query.shape
    part, kv_wide = key.shape
    heads = mesh.shape["head"]
    inners = mesh.shape["inner"]
    shards = mesh.shape["outer"] * inners
    groups = kv_wide // heads // HEAD_SIZE
    bf, f32 = jnp.bfloat16, jnp.float32
    dma = pltpu.SemaphoreType.DMA
    peers = max(heads - 1, 1)
    lanes = PAIR * HEAD_SIZE
    shapes = ((length, wide), (length, wide), (part, kv_wide), (part, kv_wide))
    half = groups // 2
    qw = GROUP * HEAD_SIZE
    block = (groups, 2, length, HEAD_SIZE)
    made = (groups, (REACH + 1) * length, qw)
    passed = (
        (length, half * qw), (length, half * qw), (groups * heads, 2, part, HEAD_SIZE),
        made, made, (REACH + 1, groups, 2, length, HEAD_SIZE),
    )
    operands = (query, key, value, output_cotangent, segment.reshape(shards, length))
    results = pl.pallas_call(
        functools.partial(kernel, inners, shards, heads),
        out_shape=tuple(pltpu.VMEM(shape, bf) for shape in passed),
        in_specs=[pl.BlockSpec(memory_space=pltpu.HBM)] * 5,
        out_specs=[pl.BlockSpec(memory_space=pltpu.VMEM)] * len(passed),
        scratch_shapes=[
            pltpu.VMEM((length, wide), bf),
            pltpu.VMEM((length, wide), bf),
            pltpu.VMEM((shards, length), jnp.int32),
            pltpu.VMEM((2, part, kv_wide), bf),
            pltpu.VMEM((groups * heads, 2, part, HEAD_SIZE), bf),
            pltpu.VMEM(block, f32),
            pltpu.VMEM(block, f32),
            pltpu.VMEM(block, bf),
            pltpu.VMEM((REACH,) + block, bf),
            pltpu.VMEM((REACH,) + block, bf),
            pltpu.VMEM(block, bf),
            pltpu.VMEM((2, length, lanes), f32),
            pltpu.VMEM((length, lanes), bf),
            dma((2, groups)),
            dma(()),
            dma((2,)),
            dma((peers,)),
            dma((peers, groups)),
            dma((REACH,)),
            dma((REACH, groups)),
            dma(()),
            dma((groups,)),
            dma((REACH,)),
            dma((REACH, groups)),
            dma((peers,)),
            dma((peers,)),
        ],
        compiler_params=pltpu.CompilerParams(
            collective_id=0, has_side_effects=True, vmem_limit_bytes=40 * 2**20
        ),
        name="packed_attention",
    )(*(pltpu.with_memory_space_constraint(x, pltpu.HBM) for x in operands))
    return pl.pallas_call(
        finish,
        out_shape=tuple(jax.ShapeDtypeStruct(shape, bf) for shape in shapes),
        in_specs=[pl.BlockSpec(memory_space=pltpu.VMEM)] * len(passed),
        out_specs=[pl.BlockSpec(memory_space=pltpu.HBM)] * 4,
        scratch_shapes=[
            pltpu.VMEM((length, wide - half * qw), bf),
            pltpu.VMEM((length, wide - half * qw), bf),
            pltpu.VMEM((2, part, kv_wide), bf),
            dma((4,)),
            dma((2, groups - half)),
        ],
        compiler_params=pltpu.CompilerParams(vmem_limit_bytes=16 * 2**20),
        name="finish",
    )(*results)


def solution(mesh):
    in_specs = (
        P(("outer", "inner"), "head"),
        P(("outer", "inner", "head"), None),
        P(("outer", "inner", "head"), None),
        P(("outer", "inner"), "head"),
        P(),
    )
    out_specs = (
        P(("outer", "inner"), "head"),
        P(("outer", "inner"), "head"),
        P(("outer", "inner", "head"), None),
        P(("outer", "inner", "head"), None),
    )
    return jax.shard_map(
        functools.partial(body, mesh),
        mesh=mesh, in_specs=in_specs, out_specs=out_specs, check_vma=False,
    )
```

```python
import functools
import math

import jax
import jax.numpy as jnp
from jax import lax
from jax.experimental import pallas as pl
from jax.experimental.pallas import tpu as pltpu
from jax.sharding import PartitionSpec as P

QUERY_HEADS = 48
KEY_VALUE_HEADS = 8
HEAD_SIZE = 128
REACH = 2
GROUP = QUERY_HEADS // KEY_VALUE_HEADS
PAIR = 2
MESH = pl.DeviceIdType.MESH


def nt(a, b):
    return lax.dot_general(a, b, (((1,), (1,)), ((), ())), preferred_element_type=jnp.float32)


def tn(a, b):
    return lax.dot_general(a, b, (((0,), (0,)), ((), ())), preferred_element_type=jnp.float32)


def nn(a, b):
    return lax.dot_general(a, b, (((1,), (0,)), ((), ())), preferred_element_type=jnp.float32)


ORDER = (0, 2, 1)


def outputs(kv, w_vm, ds_vm, att, dq, base, g, carry):
    D = HEAD_SIZE
    length = kv.shape[3]
    lanes = PAIR * D
    for t, src, dst, by in ((1, w_vm, att, None), (0, ds_vm, dq, 1.0 / math.sqrt(D))):
        flat = jnp.transpose(jnp.concatenate([kv[o, g, t] for o in ORDER], 0))
        for u in range(GROUP // PAIR):
            made = nn(flat, src[g, :, u * lanes:(u + 1) * lanes])
            if by is not None:
                made = made * by
            made = jnp.transpose(made.astype(jnp.bfloat16))
            for i in range(PAIR):
                start = (g - base) * GROUP * D + u * lanes + i * D
                dst[:, pl.ds(pl.multiple_of(start, D), D)] = made[i * length:(i + 1) * length]
    return carry


def kernel(
    inners, shards, heads,
    query_ref, key_ref, value_ref, cot_ref, seg_ref,
    att_ref, dq_ref, dkv_ref, w_vm, ds_vm, kv,
    q_vm, do_vm, seg_vm, flat_vm, own_kv, own, hold, mid, stage, got, final, bias, low,
    in_sem, seg_sem, kv_sem,
    y_send, y_recv, f_send, f_recv, r_send, m_recv, b_send, b_recv, z_send, z_recv,
):
    D = HEAD_SIZE
    length = q_vm.shape[0]
    groups = kv.shape[1]
    part = length // heads
    qw = GROUP * D
    lanes = PAIR * D
    scale = 1.0 / math.sqrt(D)
    shard = lax.axis_index("outer") * inners + lax.axis_index("inner")
    me = lax.axis_index("head")

    def at_shard(target):
        return {"outer": lax.div(target, inners), "inner": lax.rem(target, inners), "head": me}

    def at_head(target):
        return {"head": target}

    def rows(p):
        return pl.ds(pl.multiple_of(p * part, part), part)

    def cols(start, size):
        return pl.ds(pl.multiple_of(start, D), size)

    def before(j):
        return lax.rem(me + heads - j, heads)

    def after(j):
        return lax.rem(me + j, heads)

    def remote(src, dst, send, recv, target):
        return pltpu.make_async_remote_copy(
            src_ref=src, dst_ref=dst, send_sem=send, recv_sem=recv,
            device_id=target, device_id_type=MESH,
        )

    def load(g, which):
        src, dst = ((query_ref, q_vm), (cot_ref, do_vm))[which]
        c = cols(g * qw, qw)
        return pltpu.make_async_copy(src.at[:, c], dst.at[:, c], in_sem.at[which, g])

    def across(g, j):
        return remote(
            own_kv.at[after(j) * groups + g], kv.at[0, g, :, rows(me)],
            y_send.at[j - 1], y_recv.at[j - 1, g], at_head(after(j)),
        )

    def onward(g, j, o):
        r = rows(before(j))
        src = own_kv.at[me * groups + g] if j == 0 else kv.at[0, g, :, r]
        return remote(
            src, kv.at[o, g, :, r], f_send.at[o - 1], f_recv.at[o - 1, g], at_shard(shard + o)
        )

    def onward_all(g, o):
        return remote(
            kv.at[0, g], kv.at[o, g], f_send.at[o - 1], f_recv.at[o - 1, g], at_shard(shard + o)
        )

    def relay(g):
        return remote(
            kv.at[1, g], kv.at[2, g], r_send, f_recv.at[1, g], at_shard(shard + 1)
        )

    def back_near(g):
        return remote(stage.at[1, g], mid.at[g], b_send.at[1], m_recv.at[g], at_shard(shard - 1))

    def back(g, o):
        return remote(
            stage.at[o - 1, g], got.at[o - 1, g], b_send.at[o - 1], b_recv.at[o - 1, g],
            at_shard(shard - o),
        )

    def home(g, j):
        return remote(
            final.at[g, :, rows(after(j))], dkv_ref.at[me * groups + g],
            z_send.at[j - 1], z_recv.at[j - 1], at_head(after(j)),
        )

    has_next = [None] + [shard + o < shards for o in range(1, REACH + 1)]
    has_prev = [None] + [shard >= o for o in range(1, REACH + 1)]

    even = lax.rem(shard, 2) == 0
    odd = jnp.logical_not(even)
    deals_next = [None, has_next[1], jnp.logical_and(even, has_next[2])]
    deals_prev = [None, has_prev[1], jnp.logical_and(even, has_prev[2])]
    relays = deals_prev[2]

    barrier = pltpu.get_barrier_semaphore()
    for j in range(1, heads):
        pl.semaphore_signal(barrier, inc=1, device_id=at_head(after(j)), device_id_type=MESH)
    for o in range(1, REACH + 1):
        @pl.when(deals_next[o])
        def _():
            pl.semaphore_signal(barrier, inc=1, device_id=at_shard(shard + o), device_id_type=MESH)

        @pl.when(deals_prev[o])
        def _():
            pl.semaphore_signal(barrier, inc=1, device_id=at_shard(shard - o), device_id_type=MESH)

    kv_loads = [
        pltpu.make_async_copy(ref, flat_vm.at[t], kv_sem.at[t])
        for t, ref in enumerate((key_ref, value_ref))
    ]
    for copy in kv_loads:
        copy.start()
    seg_copy = pltpu.make_async_copy(seg_ref, seg_vm, seg_sem)
    seg_copy.start()
    for g in range(groups):
        for t in range(2):
            load(g, t).start()

    for t in range(2):
        kv_loads[t].wait()
        for h in range(groups * heads):
            own_kv[h, t] = flat_vm[t, :, h * D:(h + 1) * D]

    partners = heads - 1
    for o in range(1, REACH + 1):
        partners = partners + jnp.where(deals_next[o], 1, 0) + jnp.where(deals_prev[o], 1, 0)
    pl.semaphore_wait(barrier, partners)

    def share(g):
        for j in range(1, heads):
            across(g, j).start()

    def pass_own(g):
        if g < groups:
            for o in range(REACH, 0, -1):
                @pl.when(deals_next[o])
                def _():
                    onward(g, 0, o).start()

    for g in range(groups):
        share(g)
        if g < 2:
            pass_own(g)

    for g in range(groups):
        for t in range(2):
            kv[0, g, t, rows(me)] = own_kv[me * groups + g, t]
    for o in range(1, REACH + 1):
        @pl.when(jnp.logical_not(has_prev[o]))
        def _():
            kv[o] = jnp.zeros(kv.shape[1:], kv.dtype)

        @pl.when(jnp.logical_not(deals_next[o]))
        def _():
            got[o - 1] = jnp.zeros(got.shape[1:], got.dtype)

    seg_copy.wait()

    def seg_row(o):
        row = seg_vm[pl.ds(jnp.maximum(shard - o, 0), 1), :]
        return jnp.where(shard >= o, row, -1)

    def tall(row):
        return jnp.transpose(jnp.broadcast_to(row, (length, length)))

    seg_here = seg_row(0)
    key_index = lax.broadcasted_iota(jnp.int32, (length, length), 0)
    query_index = lax.broadcasted_iota(jnp.int32, (length, length), 1)
    lower = key_index <= query_index
    merged = jnp.where(lower, tall(seg_here), tall(seg_row(2)))
    blocked = -jnp.inf
    bias_own = jnp.where(merged == seg_here, 0.0, blocked)
    bias_prev = jnp.where(tall(seg_row(1)) == seg_here, 0.0, blocked)
    one_low = jnp.where(lower, 1.0, 0.0).astype(jnp.bfloat16)
    for i in range(PAIR):
        bias[0, :, i * D:(i + 1) * D] = bias_own
        bias[1, :, i * D:(i + 1) * D] = bias_prev
        low[:, i * D:(i + 1) * D] = one_low

    for g in range(groups):
        for j in range(1, heads):
            across(g, j).wait_recv()
            for o in range(REACH, 0, -1):
                @pl.when(deals_next[o])
                def _():
                    onward(g, j, o).start()
        pass_own(g + 2)

    wide_lower = lax.broadcasted_iota(jnp.int32, (length, lanes), 0) <= lax.rem(
        lax.broadcasted_iota(jnp.int32, (length, lanes), 1), D
    )

    def merge(g):
        back_near(g).wait_recv()
        stage[0, g] = (hold[g] + mid[g].astype(jnp.float32)).astype(jnp.bfloat16)
        back(g, 1).start()

    def one_group(g, carry):
        for t in range(2):
            load(g, t).wait()
        for o in range(1, REACH + 1):
            @pl.when(has_prev[o])
            def _():
                onward_all(g, o).wait_recv()

            if o == 1:
                @pl.when(relays)
                def _():
                    relay(g).start()
        keys = jnp.concatenate([kv[o, g, 0] for o in ORDER], 0)
        values = jnp.concatenate([kv[o, g, 1] for o in ORDER], 0)
        heads_q = []
        first_q = g * qw
        for u in range(GROUP // PAIR):
            spans = [cols(first_q + u * lanes + i * D, D) for i in range(PAIR)]
            q = jnp.concatenate([q_vm[:, s] for s in spans], 0)
            do = jnp.concatenate([do_vm[:, s] for s in spans], 0)
            heads_q.append((q, do, nt(keys, q), nt(values, do)))
        unit = scale * math.log2(math.e)
        for u, (q, do, scores, d_w) in enumerate(heads_q):
            s_own = jnp.where(wide_lower, scores[:length], scores[length:2 * length]) + bias[0]
            s_prev = scores[2 * length:] + bias[1]
            top = jnp.maximum(
                jnp.max(s_own, 0, keepdims=True), jnp.max(s_prev, 0, keepdims=True)
            )
            e_own = jnp.exp2((s_own - top) * unit)
            e_prev = jnp.exp2((s_prev - top) * unit)
            inv = 1.0 / (
                jnp.sum(e_own, 0, keepdims=True) + jnp.sum(e_prev, 0, keepdims=True)
            )
            w_own = e_own * inv
            w_prev = e_prev * inv
            d_own = jnp.where(wide_lower, d_w[:length], d_w[length:2 * length])
            d_prev = d_w[2 * length:]
            delta = jnp.sum(w_own * d_own, 0, keepdims=True) + jnp.sum(
                w_prev * d_prev, 0, keepdims=True
            )
            r_own = w_own.astype(jnp.bfloat16)
            g_own = (w_own * (d_own - delta)).astype(jnp.bfloat16)
            keep = low[...]
            r_low = r_own * keep
            g_low = g_own * keep
            lane = slice(u * lanes, (u + 1) * lanes)
            w_vm[g, :length, lane] = r_low
            w_vm[g, length:2 * length, lane] = r_own - r_low
            w_vm[g, 2 * length:, lane] = w_prev.astype(jnp.bfloat16)
            ds_vm[g, :length, lane] = g_low
            ds_vm[g, length:2 * length, lane] = g_own - g_low
            ds_vm[g, 2 * length:, lane] = (w_prev * (d_prev - delta)).astype(jnp.bfloat16)
        dk_sum = nn(ds_vm[g], jnp.concatenate([h[0] for h in heads_q], 0))
        dv_sum = nn(w_vm[g], jnp.concatenate([h[1] for h in heads_q], 0))
        for t, total in enumerate((dk_sum * scale, dv_sum)):
            for at, o in enumerate(ORDER):
                block = total[at * length:(at + 1) * length]
                if o == 0:
                    own[g, t] = block
                elif o == 1:
                    hold[g, t] = block
                else:
                    stage[1, g, t] = block.astype(jnp.bfloat16)

        @pl.when(relays)
        def _():
            back(g, 2).start()

            @pl.when(g >= 1)
            def _():
                merge(g - 1)

        @pl.when(jnp.logical_and(odd, has_prev[2]))
        def _():
            back_near(g).start()

        @pl.when(odd)
        def _():
            stage[0, g] = hold[g].astype(jnp.bfloat16)
            back(g, 1).start()

        return carry

    lax.fori_loop(0, groups, one_group, 0)
    lax.fori_loop(
        0, 3 * groups // 4, functools.partial(outputs, kv, w_vm, ds_vm, att_ref, dq_ref, 0), 0
    )

    @pl.when(relays)
    def _():
        merge(groups - 1)

    for g in range(groups):
        for o in range(1, REACH + 1):
            @pl.when(deals_next[o])
            def _():
                back(g, o).wait_recv()
        total = own[g]
        for o in range(1, REACH + 1):
            total = total + got[o - 1, g].astype(jnp.float32)
        final[g] = total.astype(jnp.bfloat16)
        for j in range(1, heads):
            home(g, j).start()
        dkv_ref[me * groups + g] = final[g, :, rows(me)]

    for j in range(1, heads):
        share = own_kv.at[pl.ds(0, groups)]
        remote(share, share, y_send.at[j - 1], y_recv.at[j - 1, 0], at_head(after(j))).wait_send()
        landed = dkv_ref.at[pl.ds(0, groups)]
        ends = remote(share, landed, z_send.at[j - 1], z_recv.at[j - 1], at_head(after(j)))
        ends.wait_send()
        ends.wait_recv()
    for o in range(1, REACH + 1):
        @pl.when(deals_next[o])
        def _():
            remote(
                kv.at[0], kv.at[o], f_send.at[o - 1], f_recv.at[o - 1, 0], at_shard(shard + o)
            ).wait_send()

        @pl.when(has_prev[o])
        def _():
            remote(
                stage.at[o - 1], got.at[o - 1], b_send.at[o - 1], b_recv.at[o - 1, 0],
                at_shard(shard - o),
            ).wait_send()

    @pl.when(relays)
    def _():
        remote(kv.at[1], kv.at[2], r_send, f_recv.at[1, 0], at_shard(shard + 1)).wait_send()


def finish(
    att_a, dq_a, dkv, w_vm, ds_vm, kv, att_out, dq_out, dk_out, dv_out,
    att_b, dq_b, flat, sems, late
):
    groups = w_vm.shape[0]
    half = 3 * groups // 4
    qw = GROUP * HEAD_SIZE
    early = pl.ds(0, half * qw)
    copies = []
    for i, (src, dst) in enumerate((
        (att_a, att_out.at[:, early]), (dq_a, dq_out.at[:, early]),
        (flat.at[0], dk_out), (flat.at[1], dv_out),
    )):
        if i >= 2:
            for h in range(dkv.shape[0]):
                flat[i - 2, :, h * HEAD_SIZE:(h + 1) * HEAD_SIZE] = dkv[h, i - 2]
        copies.append(pltpu.make_async_copy(src, dst, sems.at[i]))
        copies[-1].start()

    for g in range(half, groups):
        outputs(kv, w_vm, ds_vm, att_b, dq_b, half, g, 0)
        here, there = pl.ds((g - half) * qw, qw), pl.ds(g * qw, qw)
        for t, (src, dst) in enumerate(((att_b, att_out), (dq_b, dq_out))):
            copies.append(
                pltpu.make_async_copy(src.at[:, here], dst.at[:, there], late.at[t, g - half])
            )
            copies[-1].start()
    for copy in copies:
        copy.wait()


def body(mesh, query, key, value, output_cotangent, segment):
    length, wide = query.shape
    part, kv_wide = key.shape
    heads = mesh.shape["head"]
    inners = mesh.shape["inner"]
    shards = mesh.shape["outer"] * inners
    groups = kv_wide // heads // HEAD_SIZE
    bf, f32 = jnp.bfloat16, jnp.float32
    dma = pltpu.SemaphoreType.DMA
    peers = max(heads - 1, 1)
    lanes = PAIR * HEAD_SIZE
    shapes = ((length, wide), (length, wide), (part, kv_wide), (part, kv_wide))
    half = 3 * groups // 4
    qw = GROUP * HEAD_SIZE
    block = (groups, 2, length, HEAD_SIZE)
    made = (groups, (REACH + 1) * length, qw)
    passed = (
        (length, half * qw), (length, half * qw), (groups * heads, 2, part, HEAD_SIZE),
        made, made, (REACH + 1, groups, 2, length, HEAD_SIZE),
    )
    operands = (query, key, value, output_cotangent, segment.reshape(shards, length))
    results = pl.pallas_call(
        functools.partial(kernel, inners, shards, heads),
        out_shape=tuple(pltpu.VMEM(shape, bf) for shape in passed),
        in_specs=[pl.BlockSpec(memory_space=pltpu.HBM)] * 5,
        out_specs=[pl.BlockSpec(memory_space=pltpu.VMEM)] * len(passed),
        scratch_shapes=[
            pltpu.VMEM((length, wide), bf),
            pltpu.VMEM((length, wide), bf),
            pltpu.VMEM((shards, length), jnp.int32),
            pltpu.VMEM((2, part, kv_wide), bf),
            pltpu.VMEM((groups * heads, 2, part, HEAD_SIZE), bf),
            pltpu.VMEM(block, f32),
            pltpu.VMEM(block, f32),
            pltpu.VMEM(block, bf),
            pltpu.VMEM((REACH,) + block, bf),
            pltpu.VMEM((REACH,) + block, bf),
            pltpu.VMEM(block, bf),
            pltpu.VMEM((2, length, lanes), f32),
            pltpu.VMEM((length, lanes), bf),
            dma((2, groups)),
            dma(()),
            dma((2,)),
            dma((peers,)),
            dma((peers, groups)),
            dma((REACH,)),
            dma((REACH, groups)),
            dma(()),
            dma((groups,)),
            dma((REACH,)),
            dma((REACH, groups)),
            dma((peers,)),
            dma((peers,)),
        ],
        compiler_params=pltpu.CompilerParams(
            collective_id=0, has_side_effects=True, vmem_limit_bytes=40 * 2**20
        ),
        name="packed_attention",
    )(*(pltpu.with_memory_space_constraint(x, pltpu.HBM) for x in operands))
    return pl.pallas_call(
        finish,
        out_shape=tuple(jax.ShapeDtypeStruct(shape, bf) for shape in shapes),
        in_specs=[pl.BlockSpec(memory_space=pltpu.VMEM)] * len(passed),
        out_specs=[pl.BlockSpec(memory_space=pltpu.HBM)] * 4,
        scratch_shapes=[
            pltpu.VMEM((length, wide - half * qw), bf),
            pltpu.VMEM((length, wide - half * qw), bf),
            pltpu.VMEM((2, part, kv_wide), bf),
            dma((4,)),
            dma((2, groups - half)),
        ],
        compiler_params=pltpu.CompilerParams(vmem_limit_bytes=16 * 2**20),
        name="finish",
    )(*results)


def solution(mesh):
    in_specs = (
        P(("outer", "inner"), "head"),
        P(("outer", "inner", "head"), None),
        P(("outer", "inner", "head"), None),
        P(("outer", "inner"), "head"),
        P(),
    )
    out_specs = (
        P(("outer", "inner"), "head"),
        P(("outer", "inner"), "head"),
        P(("outer", "inner", "head"), None),
        P(("outer", "inner", "head"), None),
    )
    return jax.shard_map(
        functools.partial(body, mesh),
        mesh=mesh, in_specs=in_specs, out_specs=out_specs, check_vma=False,
    )
```
